512 devices in a mesh: gen: 2 (over z_hi), row: 64 (over z_lo, x, core), col: 4 (over y).
Axes of the slice: x: 4, y: 4, z: 16 (z_hi: 2, z_lo: 8; z = z_hi * 8 + z_lo), core: 2. Of those that a mesh axis runs over, the one named last changes fastest.
Arguments:
- coords: int32 [2, 65536], P(None, 'row'), may hold values from 0 to 1023
- factor: float32 [65536, 8192], P('row', ('gen', 'col')), as said below
Outputs:
- panel_factor: float32 [65536, 512], P('row', ('gen', 'col'))
The draws below stay inside these ranges and needn't reach their ends.
Inputs may be any that keep to these rules, and one draw needn't show every extreme that they name: `factor`: the kernel at the panel's points minus panel_rows panel_rows^T is positive definite.
All inputs are finite; a program needn't handle non-finite values.
Results may differ from the reference program's by a relative error of at most 0.0003.
Values sent between devices are 32-bit elements; how exact they have to be, the bound alone decides.
A program may use at most 64 MiB of HBM per device.

```python
import jax
import jax.numpy as jnp
from jax import lax

B = 512
ROW_DEV = 1024
GRID = 1024
M = 65536
K = 8192
PAN_DEV = 8
N_ROW = 64


def grid_coords(key):
    return jax.random.randint(key, (2, M), 0, GRID, jnp.int32)


def draw_coords(key, part):
    return grid_coords(key)


def draw_factor(key, part):
    coords = grid_coords(key)
    key = jax.random.fold_in(key, 5)
    normal_key = jax.random.fold_in(key, 1)
    chi_key = jax.random.fold_in(key, 2)
    phase_key = jax.random.fold_in(key, 3)
    normals = jax.random.normal(normal_key, (2, K), jnp.float32)
    chi_parts = jax.random.normal(chi_key, (3, K), jnp.float32)
    chi_square = chi_parts[0] * chi_parts[0] + chi_parts[1] * chi_parts[1] + chi_parts[2] * chi_parts[2]
    stretch = 1.0 / (0.2 * jnp.sqrt(jnp.maximum(chi_square, 0.3) / 3.0))
    frequency = normals * stretch[None, :]
    phases = jax.random.uniform(phase_key, (K,), jnp.float32, 0.0, 6.283185307179586)
    points = coords.astype(jnp.float32) / GRID
    fraction = 0.6 / (1.0 + (B / K) ** 0.5) ** 2
    amplitude = (2.0 * fraction / K) ** 0.5
    angles = points[0][:, None] * frequency[0][None, :] + points[1][:, None] * frequency[1][None, :] + phases[None, :]
    values = amplitude * jnp.cos(angles)
    return values


def setup_inputs(seed: int = 0) -> dict:
    streams_of = jax.random.split(jax.random.key(seed), 3)
    coords = draw_coords(jax.random.fold_in(streams_of[2], 71), 0)
    factor = draw_factor(jax.random.fold_in(streams_of[2], 71), 0)
    return {"coords": coords, "factor": factor}


root_three = 1.7320508075688772
length_scale = 0.2
nugget_term = 1.0

def panel_kernel(row_points, col_points, row_ids, col_ids):
    delta_x = row_points[0][:, None] - col_points[0][None, :]
    delta_y = row_points[1][:, None] - col_points[1][None, :]
    scaled = root_three * jnp.sqrt(delta_x * delta_x + delta_y * delta_y) / length_scale
    same = jnp.where(row_ids[:, None] == col_ids[None, :], jnp.float32(nugget_term), jnp.float32(0.0))
    return (1.0 + scaled) * jnp.exp(-scaled) + same

def reference(coords, factor):
    points = coords.astype(jnp.float32) / GRID
    panel_points = points.reshape(2, N_ROW, ROW_DEV)[:, :, :PAN_DEV].reshape(2, B)
    panel_rows = factor.reshape(N_ROW, ROW_DEV, K)[:, :PAN_DEV].reshape(B, K)
    row_ids = jnp.arange(M, dtype=jnp.int32)
    columns = jnp.arange(B, dtype=jnp.int32)
    col_ids = columns // PAN_DEV * ROW_DEV + columns % PAN_DEV
    update = lax.dot_general(factor.astype(jnp.float32), panel_rows.astype(jnp.float32), (((1,), (1,)), ((), ())), precision=lax.Precision.HIGHEST, preferred_element_type=jnp.float32)
    updated = panel_kernel(points, panel_points, row_ids, col_ids) - update
    diagonal_block = updated.reshape(N_ROW, ROW_DEV, B)[:, :PAN_DEV].reshape(B, B)
    lower = jnp.linalg.cholesky(diagonal_block)
    return lax.linalg.triangular_solve(lower, updated, left_side=False, lower=True, transpose_a=True)
```

```python
import jax
import jax.numpy as jnp
from jax import lax
from jax.experimental import pallas as pl
from jax.experimental.pallas import tpu as pltpu
from jax.sharding import PartitionSpec as P

B = 512
GRID = 1024
PAN = 8
ROWS = 1024
DEPTH = 1024
QUART = 256
NZ, NX, NC, NCOL = 8, 4, 2, 4
WIDE = DEPTH + 128

root_three = 1.7320508075688772
length_scale = 0.2
nugget_term = 1.0

HI = lax.Precision.HIGHEST
MESH = pl.DeviceIdType.MESH


def dotf(a, b, dims):
    return lax.dot_general(a, b, (dims, ((), ())), precision=HI, preferred_element_type=jnp.float32)


def matern(delta_x, delta_y):
    scaled = root_three * jnp.sqrt(delta_x * delta_x + delta_y * delta_y) / length_scale
    return (1.0 + scaled) * jnp.exp(-scaled)


def spread(x, k):
    return jnp.broadcast_to(x[k : k + 1], x.shape)


def inverse_factor(tile_ref, out_ref):
    sub = lax.broadcasted_iota(jnp.int32, (8, 128), 0)
    lane = lax.broadcasted_iota(jnp.int32, (8, 128), 1)
    a = [tile_ref[8 * i : 8 * i + 8, :] for i in range(16)]
    t = [jnp.where(lane == sub + 8 * i, jnp.float32(1), jnp.float32(0)) for i in range(16)]
    for b in range(16):
        cols = [jnp.broadcast_to(a[b][:, 8 * b + k : 8 * b + k + 1], (8, 128)) for k in range(8)]
        recip, cross, scale = [], [], jnp.ones((8, 128), jnp.float32)
        for k in range(8):
            pivot = spread(cols[k], k)
            r = 1.0 / pivot
            recip.append(r)
            scale = jnp.where(sub == k, pivot, scale)
            m = jnp.where(sub > k, cols[k] * r, 0.0)
            row = []
            for j in range(k + 1, 8):
                s = spread(cols[j], k)
                row.append(s)
                cols[j] = cols[j] - m * s
            cross.append(row)
            a[b] = a[b] - m * spread(a[b], k)
            t[b] = t[b] - m * spread(t[b], k)
        ua = [spread(a[b], k) for k in range(8)]
        ut = [spread(t[b], k) for k in range(8)]
        out_ref[8 * b : 8 * b + 8, :] = t[b] * lax.rsqrt(scale)
        for i in range(b + 1, 16):
            c = [jnp.broadcast_to(a[i][:, 8 * b + k : 8 * b + k + 1], (8, 128)) for k in range(8)]
            da = dt = None
            for k in range(8):
                m = c[k] * recip[k]
                for j in range(k + 1, 8):
                    c[j] = c[j] - m * cross[k][j - k - 1]
                da = m * ua[k] if da is None else da + m * ua[k]
                dt = m * ut[k] if dt is None else dt + m * ut[k]
            a[i] = a[i] - da
            t[i] = t[i] - dt


def place():
    h, r, c = lax.axis_index("gen"), lax.axis_index("row"), lax.axis_index("col")
    return h, r, c, r // 8, (r // 2) % 4, r % 2


def send(src, dst, send_sem, recv_sem, where):
    return pltpu.make_async_remote_copy(
        src_ref=src, dst_ref=dst, send_sem=send_sem, recv_sem=recv_sem, device_id=where, device_id_type=MESH
    )


class Gather:
    def __init__(self, buf, sz, rz, sx, rx, sc, rc):
        self.buf, self.sz, self.rz, self.sx, self.rx, self.sc, self.rc = buf, sz, rz, sx, rx, sc, rc
        _, self.r, _, self.z, self.x, self.core = place()

    def along_z(self, source, d):
        target = (self.z + d) % NZ
        block = self.buf.at[source, self.x, self.core]
        return send(block, block, self.sz.at[d - 1], self.rz.at[source], {"row": target * 8 + self.x * 2 + self.core})

    def along_x(self, source, e):
        target = (self.x + e) % NX
        block = self.buf.at[source, self.x, self.core]
        return send(block, block, self.sx.at[source, e - 1], self.rx.at[source, self.x],
                    {"row": self.z * 8 + target * 2 + self.core})

    def from_x(self, source, e):
        x = (self.x + e) % NX
        block = self.buf.at[source, x, self.core]
        return send(block, block, self.sx.at[source, 0], self.rx.at[source, x], {"row": self.r + 1 - 2 * self.core})

    def across(self, source, core):
        block = self.buf.at[source, :, core]
        return send(block, block, self.sc.at[source], self.rc.at[source], {"row": self.r + 1 - 2 * self.core})

    def run(self):
        z = self.z
        for d in range(1, NZ):
            self.along_z(z, d).start()
        for e in range(1, NX):
            self.along_x(z, e).start()

        def forward(d, carry):
            source = (z + NZ - d) % NZ
            self.along_z(source, 1).wait_recv()
            for e in range(1, NX):
                self.along_x(source, e).start()
            return carry

        lax.fori_loop(1, NZ, forward, 0)

        def swap(d, carry):
            source = (z + NZ - d) % NZ
            for e in range(1, NX):
                self.from_x(source, e).wait_recv()
            self.across(source, self.core).start()
            return carry

        lax.fori_loop(0, NZ, swap, 0)

        def arrive(source, carry):
            self.across(source, 1 - self.core).wait_recv()
            return carry

        lax.fori_loop(0, NZ, arrive, 0)

    def finish(self):
        for d in range(1, NZ):
            self.along_z(self.z, d).wait_send()

        def drain(source, carry):
            for e in range(1, NX):
                self.along_x(source, e).wait_send()
            self.across(source, self.core).wait_send()
            return carry

        lax.fori_loop(0, NZ, drain, 0)


def gather_sems():
    dma = pltpu.SemaphoreType.DMA
    return [dma((NZ - 1,)), dma((NZ,)), dma((NZ, NX - 1)), dma((NZ, NX)), dma((NZ,)), dma((NZ,))]


def greet():
    h, r, c, z, x, core = place()
    barrier = pltpu.get_barrier_semaphore()
    peers = [{"row": (z + d) % NZ * 8 + x * 2 + core} for d in range(1, NZ)]
    peers += [{"row": z * 8 + (x + e) % NX * 2 + core} for e in range(1, NX)]
    peers += [{"row": r + 1 - 2 * core}]
    peers += [{"col": (c + e) % NCOL} for e in range(1, NCOL)]
    peers += [{"gen": 1 - h}]
    for peer in peers:
        pl.semaphore_signal(barrier, inc=1, device_id=peer, device_id_type=MESH)
    pl.semaphore_wait(barrier, len(peers))


def front_kernel(factor, lanes, mine, diag, points, bulk, fv, pan, u, dgat, dy, dg, ybuf, local, sdy, rdy, sdg, rdg, sy, ry, *sems):
    h, r, c, z, x, core = place()
    load = pltpu.make_async_copy(factor, fv, local.at[0])
    rows = pltpu.make_async_copy(factor.at[pl.ds(0, PAN), :], pan.at[z, x, core, :, pl.ds(0, DEPTH)], local.at[1])
    marks = pltpu.make_async_copy(lanes, pan.at[z, x, core, :, pl.ds(DEPTH, 128)], local.at[2])
    rows.start()
    marks.start()
    load.start()
    greet()
    rows.wait()
    marks.wait()
    first = Gather(pan, *sems[:6])
    second = Gather(dgat, *sems[6:])
    first.run()
    load.wait()

    def y_small(e):
        return send(u.at[pl.ds(0, PAN), :], dy.at[e - 1], sdy.at[e - 1], rdy.at[e - 1], {"col": (c + e) % NCOL})

    def y_large(e):
        part = (c + e) % NCOL
        return send(u.at[pl.ds(part * QUART, QUART), :], ybuf.at[e - 1], sy.at[e - 1], ry.at[e - 1], {"col": part})

    gen_small = send(dy.at[NCOL - 1], dg, sdg.at[0], rdg.at[0], {"gen": 1 - h})

    def multiply(q, carry):
        at = pl.ds(pl.multiple_of(q * QUART, QUART), QUART)
        panel = pan[:, :, :, :, :DEPTH].reshape(B, DEPTH)
        u[at, :] = dotf(fv[at, :], panel, ((1,), (1,)))

        @pl.when(q == 0)
        def _():
            for e in range(1, NCOL):
                y_small(e).start()

        return carry

    lax.fori_loop(0, NCOL, multiply, 0)
    for e in range(1, NCOL):
        y_small(e).wait_recv()
    dy[NCOL - 1] = u[:PAN, :] + dy[0] + dy[1] + dy[2]
    gen_small.start()
    for e in range(1, NCOL):
        y_large(e).start()
    marks8 = pan[:, :, :, :, DEPTH:].reshape(4, 16, PAN, 128)
    for q in range(4):
        total = marks8[q, 0]
        for i in range(1, 16):
            total = total + marks8[q, i]
        points[:, 128 * q : 128 * q + 128] = total
    px = jnp.broadcast_to(mine[:, :1], (PAN, B))
    py = jnp.broadcast_to(mine[:, 128:129], (PAN, B))
    sub = lax.broadcasted_iota(jnp.int32, (PAN, B), 0)
    lane = lax.broadcasted_iota(jnp.int32, (PAN, B), 1)
    same = jnp.where(lane == sub + PAN * r, jnp.float32(nugget_term), jnp.float32(0))
    kern = matern(px - points[0:1, :], py - points[1:2, :]) + same
    gen_small.wait_recv()
    dgat[z, x, core] = kern - (dy[NCOL - 1] + dg[...])
    second.run()
    diag[...] = dgat[...].reshape(B, B)
    for e in range(1, NCOL):
        y_large(e).wait_recv()
    here = pl.ds(pl.multiple_of(c * QUART, QUART), QUART)
    bulk[...] = u[here, :] + ybuf[0] + ybuf[1] + ybuf[2]
    for e in range(1, NCOL):
        y_small(e).wait_send()
        y_large(e).wait_send()
    gen_small.wait_send()
    first.finish()
    second.finish()


def front(factor, lanes, mine):
    dma = pltpu.SemaphoreType.DMA
    f32 = jnp.float32
    vmem = pl.BlockSpec(memory_space=pltpu.VMEM)
    return pl.pallas_call(
        front_kernel,
        out_shape=[
            jax.ShapeDtypeStruct((B, B), f32),
            jax.ShapeDtypeStruct((PAN, B), f32),
            jax.ShapeDtypeStruct((QUART, B), f32),
        ],
        in_specs=[pl.BlockSpec(memory_space=pl.ANY), vmem, vmem],
        out_specs=[vmem, vmem, vmem],
        scratch_shapes=[
            pltpu.VMEM((ROWS, DEPTH), f32),
            pltpu.VMEM((NZ, NX, NC, PAN, WIDE), f32),
            pltpu.VMEM((ROWS, B), f32),
            pltpu.VMEM((NZ, NX, NC, PAN, B), f32),
            pltpu.VMEM((NCOL, PAN, B), f32),
            pltpu.VMEM((PAN, B), f32),
            pltpu.VMEM((NCOL - 1, QUART, B), f32),
            dma((3,)), dma((3,)), dma((3,)), dma((1,)), dma((1,)), dma((3,)), dma((3,)),
            *gather_sems(), *gather_sems(),
        ],
        compiler_params=pltpu.CompilerParams(
            collective_id=0, has_side_effects=True, vmem_limit_bytes=48 << 20
        ),
        name="front",
    )(factor, lanes, mine)


def chol_kernel(d_ref, out_ref, work, tile, inv):
    n = 4
    work[...] = d_ref[...]
    out_ref[...] = jnp.zeros((B, B), jnp.float32)

    def step(k, carry):
        for v in range(n):
            @pl.when(k == v)
            def _():
                tile[...] = work[128 * v : 128 * v + 128, 128 * v : 128 * v + 128]
        inverse_factor(tile, inv)
        for v in range(n):
            @pl.when(k == v)
            def _():
                lo, hi = 128 * v, 128 * v + 128
                t = inv[...]
                if v:
                    out_ref[lo:hi, :lo] = dotf(t, out_ref[lo:hi, :lo], ((1,), (0,)))
                out_ref[lo:hi, lo:hi] = t
                if v < n - 1:
                    r = dotf(t, work[lo:hi, hi:], ((1,), (0,)))
                    work[hi:, hi:] = work[hi:, hi:] - dotf(r, r, ((0,), (0,)))
                    out_ref[hi:, :hi] = out_ref[hi:, :hi] - dotf(r, out_ref[lo:hi, :hi], ((0,), (0,)))
        return carry

    lax.fori_loop(0, n, step, 0)


def inverse_lower(d):
    vmem = pl.BlockSpec(memory_space=pltpu.VMEM)
    return pl.pallas_call(
        chol_kernel,
        out_shape=jax.ShapeDtypeStruct((B, B), jnp.float32),
        in_specs=[vmem],
        out_specs=vmem,
        scratch_shapes=[
            pltpu.VMEM((B, B), jnp.float32),
            pltpu.VMEM((128, 128), jnp.float32),
            pltpu.VMEM((128, 128), jnp.float32),
        ],
        compiler_params=pltpu.CompilerParams(vmem_limit_bytes=16 << 20),
        cost_estimate=pl.CostEstimate(flops=200_000_000_000, bytes_accessed=2 << 20, transcendentals=0),
        name="inverse_lower",
    )(d)


def shards(coords, factor):
    h, r, c = lax.axis_index("gen"), lax.axis_index("row"), lax.axis_index("col")
    points = coords.astype(jnp.float32) / GRID
    lane = lax.broadcasted_iota(jnp.int32, (PAN, 128), 1)
    sub = lax.broadcasted_iota(jnp.int32, (PAN, 128), 0)
    lanes = jnp.zeros((PAN, 128), jnp.float32)
    for j in range(PAN):
        value = jnp.where(sub == 0, points[0, j], jnp.where(sub == 1, points[1, j], 0.0))
        lanes = jnp.where(lane == (r % 16) * PAN + j, value, lanes)
    mine = jnp.broadcast_to(points[:, :PAN].T[:, :, None], (PAN, 2, 128)).reshape(PAN, 256)
    diag, pan_points, bulk = front(factor, lanes, mine)
    other = lax.ppermute(bulk, "gen", [(0, 1), (1, 0)])
    inverse = inverse_lower(diag)
    here = lax.dynamic_slice_in_dim(points, c * QUART, QUART, 1)
    ids = c * QUART + jnp.arange(QUART, dtype=jnp.int32)
    columns = jnp.arange(B, dtype=jnp.int32)
    same = (ids[:, None] < PAN) & (columns[None, :] == r * PAN + ids[:, None])
    kern = matern(here[0][:, None] - pan_points[0][None, :], here[1][:, None] - pan_points[1][None, :])
    kern = kern + jnp.where(same, jnp.float32(nugget_term), jnp.float32(0.0))
    updated = kern - (bulk + other)
    wanted = lax.dynamic_slice_in_dim(inverse, h * 256, 256, 0)
    solved = dotf(updated, wanted, ((1,), (1,)))
    blocks = []
    for e in range(NCOL):
        part = lax.dynamic_slice_in_dim(solved, (c + e) % NCOL * 64, 64, 1)
        blocks.append(lax.ppermute(part, "col", [(i, (i + e) % NCOL) for i in range(NCOL)]) if e else part)
    out = jnp.zeros((ROWS, 64), jnp.float32)
    for e in range(NCOL):
        out = lax.dynamic_update_slice_in_dim(out, blocks[e], (c + NCOL - e) % NCOL * QUART, 0)
    return out


def solution(mesh):
    in_specs = (P(None, "row"), P("row", ("gen", "col")))
    out_specs = P("row", ("gen", "col"))
    return jax.shard_map(shards, mesh=mesh, in_specs=in_specs, out_specs=out_specs, check_vma=False)
```

```python
import jax
import jax.numpy as jnp
from jax import lax
from jax.experimental import pallas as pl
from jax.experimental.pallas import tpu as pltpu
from jax.sharding import PartitionSpec as P

B = 512
GRID = 1024
PAN = 8
ROWS = 1024
DEPTH = 1024
HALF = 128
NZ, NX, NC, NCOL = 8, 4, 2, 4
WIDE = DEPTH + 128

root_three = 1.7320508075688772
length_scale = 0.2
nugget_term = 1.0

HI = lax.Precision.HIGHEST
MESH = pl.DeviceIdType.MESH


def dotf(a, b, dims):
    return lax.dot_general(a, b, (dims, ((), ())), precision=HI, preferred_element_type=jnp.float32)


def matern(delta_x, delta_y):
    scaled = root_three * jnp.sqrt(delta_x * delta_x + delta_y * delta_y) / length_scale
    return (1.0 + scaled) * jnp.exp(-scaled)


def spread(x, k):
    return jnp.broadcast_to(x[k : k + 1], x.shape)


def inverse_factor(tile_ref, out_ref):
    sub = lax.broadcasted_iota(jnp.int32, (8, 128), 0)
    lane = lax.broadcasted_iota(jnp.int32, (8, 128), 1)
    a = [tile_ref[8 * i : 8 * i + 8, :] for i in range(16)]
    t = [jnp.where(lane == sub + 8 * i, jnp.float32(1), jnp.float32(0)) for i in range(16)]
    for b in range(16):
        cols = [jnp.broadcast_to(a[b][:, 8 * b + k : 8 * b + k + 1], (8, 128)) for k in range(8)]
        recip, cross, scale = [], [], jnp.ones((8, 128), jnp.float32)
        for k in range(8):
            pivot = spread(cols[k], k)
            r = 1.0 / pivot
            recip.append(r)
            scale = jnp.where(sub == k, pivot, scale)
            m = jnp.where(sub > k, cols[k] * r, 0.0)
            row = []
            for j in range(k + 1, 8):
                s = spread(cols[j], k)
                row.append(s)
                cols[j] = cols[j] - m * s
            cross.append(row)
            a[b] = a[b] - m * spread(a[b], k)
            t[b] = t[b] - m * spread(t[b], k)
        ua = [spread(a[b], k) for k in range(8)]
        ut = [spread(t[b], k) for k in range(8)]
        out_ref[8 * b : 8 * b + 8, :] = t[b] * lax.rsqrt(scale)
        for i in range(b + 1, 16):
            c = [jnp.broadcast_to(a[i][:, 8 * b + k : 8 * b + k + 1], (8, 128)) for k in range(8)]
            da = dt = None
            for k in range(8):
                m = c[k] * recip[k]
                for j in range(k + 1, 8):
                    c[j] = c[j] - m * cross[k][j - k - 1]
                da = m * ua[k] if da is None else da + m * ua[k]
                dt = m * ut[k] if dt is None else dt + m * ut[k]
            a[i] = a[i] - da
            t[i] = t[i] - dt


def place():
    h, r, c = lax.axis_index("gen"), lax.axis_index("row"), lax.axis_index("col")
    return h, r, c, r // 8, (r // 2) % 4, r % 2


def send(src, dst, send_sem, recv_sem, where):
    return pltpu.make_async_remote_copy(
        src_ref=src, dst_ref=dst, send_sem=send_sem, recv_sem=recv_sem, device_id=where, device_id_type=MESH
    )


class Gather:
    def __init__(self, buf, sz, rz, sx, rx, sc, rc):
        self.buf, self.sz, self.rz, self.sx, self.rx, self.sc, self.rc = buf, sz, rz, sx, rx, sc, rc
        _, self.r, _, self.z, self.x, self.core = place()

    def along_z(self, source, d):
        target = (self.z + d) % NZ
        block = self.buf.at[source, self.x, self.core]
        return send(block, block, self.sz.at[d - 1], self.rz.at[source], {"row": target * 8 + self.x * 2 + self.core})

    def along_x(self, source, e):
        target = (self.x + e) % NX
        block = self.buf.at[source, self.x, self.core]
        return send(block, block, self.sx.at[source, e - 1], self.rx.at[source, self.x],
                    {"row": self.z * 8 + target * 2 + self.core})

    def from_x(self, source, e):
        x = (self.x + e) % NX
        block = self.buf.at[source, x, self.core]
        return send(block, block, self.sx.at[source, 0], self.rx.at[source, x], {"row": self.r + 1 - 2 * self.core})

    def across(self, source, core):
        block = self.buf.at[source, :, core]
        return send(block, block, self.sc.at[source], self.rc.at[source], {"row": self.r + 1 - 2 * self.core})

    def run(self):
        z = self.z
        for d in range(1, NZ):
            self.along_z(z, d).start()
        for e in range(1, NX):
            self.along_x(z, e).start()

        def forward(d, carry):
            source = (z + NZ - d) % NZ
            self.along_z(source, 1).wait_recv()
            for e in range(1, NX):
                self.along_x(source, e).start()
            return carry

        lax.fori_loop(1, NZ, forward, 0)

        def swap(d, carry):
            source = (z + NZ - d) % NZ
            for e in range(1, NX):
                self.from_x(source, e).wait_recv()
            self.across(source, self.core).start()
            return carry

        lax.fori_loop(0, NZ, swap, 0)

        def arrive(source, carry):
            self.across(source, 1 - self.core).wait_recv()
            return carry

        lax.fori_loop(0, NZ, arrive, 0)

    def finish(self):
        for d in range(1, NZ):
            self.along_z(self.z, d).wait_send()

        def drain(source, carry):
            for e in range(1, NX):
                self.along_x(source, e).wait_send()
            self.across(source, self.core).wait_send()
            return carry

        lax.fori_loop(0, NZ, drain, 0)


def gather_sems():
    dma = pltpu.SemaphoreType.DMA
    return [dma((NZ - 1,)), dma((NZ,)), dma((NZ, NX - 1)), dma((NZ, NX)), dma((NZ,)), dma((NZ,))]


def greet():
    h, r, c, z, x, core = place()
    barrier = pltpu.get_barrier_semaphore()
    peers = [{"row": (z + d) % NZ * 8 + x * 2 + core} for d in range(1, NZ)]
    peers += [{"row": z * 8 + (x + e) % NX * 2 + core} for e in range(1, NX)]
    peers += [{"row": r + 1 - 2 * core}]
    peers += [{"col": (c + e) % NCOL} for e in range(1, NCOL)]
    peers += [{"gen": 1 - h, "col": (c + e) % NCOL} for e in range(NCOL)]
    for peer in peers:
        pl.semaphore_signal(barrier, inc=1, device_id=peer, device_id_type=MESH)
    pl.semaphore_wait(barrier, len(peers))


def halves(x):
    high = x.astype(jnp.bfloat16)
    return high, (x - high.astype(jnp.float32)).astype(jnp.bfloat16)


def three(a, b):
    dims = (((1,), (1,)), ((), ()))
    f32 = jnp.float32
    total = lax.dot_general(a[0], b[1], dims, preferred_element_type=f32)
    total += lax.dot_general(a[1], b[0], dims, preferred_element_type=f32)
    return total + lax.dot_general(a[0], b[0], dims, preferred_element_type=f32)


def step_kernel(
    coords, factor, out, fv, pan, high, low, u, dgat, dy, dg, ybuf, gout, gbuf, marks, points, upd,
    work, tile, inv, linv, xs, xt, local, sdy, rdy, sdg, rdg, sy, ry, sg, rg, sx, rx, *sems,
):
    h, r, c, z, x, core = place()
    f32 = jnp.float32
    load = pltpu.make_async_copy(factor, fv, local.at[0])
    rows = pltpu.make_async_copy(factor.at[0, 0, pl.ds(0, PAN), :], pan.at[z, x, core, :, pl.ds(0, DEPTH)], local.at[1])
    rows.start()
    load.start()

    sub = lax.broadcasted_iota(jnp.int32, (PAN, 128), 0)
    lane = lax.broadcasted_iota(jnp.int32, (PAN, 128), 1)
    start = coords[:, :128].astype(f32) / GRID
    mark = jnp.zeros((PAN, 128), f32)
    own_x, own_y = mark, mark
    for j in range(PAN):
        px = jnp.broadcast_to(start[0:1, j : j + 1], (PAN, 128))
        py = jnp.broadcast_to(start[1:2, j : j + 1], (PAN, 128))
        own_x = jnp.where(sub == j, px, own_x)
        own_y = jnp.where(sub == j, py, own_y)
        both = jnp.where(sub == 0, px, jnp.where(sub == 1, py, 0.0))
        mark = jnp.where(lane == (r % 16) * PAN + j, both, mark)
    marks[...] = mark
    tag = pltpu.make_async_copy(marks, pan.at[z, x, core, :, pl.ds(DEPTH, 128)], local.at[2])
    tag.start()
    greet()
    rows.wait()
    tag.wait()
    first = Gather(pan, *sems[:6])
    second = Gather(dgat, *sems[6:])
    first.run()
    load.wait()

    def y_small(e):
        return send(u.at[0, 0, pl.ds(0, PAN), :], dy.at[e - 1], sdy.at[e - 1], rdy.at[e - 1], {"col": (c + e) % NCOL})

    def y_large(s, e):
        part = (c + e) % NCOL
        return send(u.at[part, s], ybuf.at[s, e - 1], sy.at[s, e - 1], ry.at[s, e - 1], {"col": part})

    gen_small = send(dy.at[NCOL - 1], dg, sdg.at[0], rdg.at[0], {"gen": 1 - h})
    gen_large = send(gout, gbuf, sg.at[0], rg.at[0], {"gen": 1 - h})

    high[...], low[...] = halves(pan[:, :, :, :, :DEPTH].reshape(B, DEPTH))

    def multiply(s):
        a = halves(fv[:, s].reshape(4 * HALF, DEPTH))
        u[:, s] = three(a, (high[...], low[...])).reshape(4, HALF, B)

    multiply(0)
    for e in range(1, NCOL):
        y_small(e).start()

    @pl.when(h == 1)
    def _():
        for e in range(1, NCOL):
            y_large(0, e).start()

    multiply(1)

    for e in range(1, NCOL):
        y_small(e).wait_recv()
    dy[NCOL - 1] = u[0, 0, :PAN, :] + dy[0] + dy[1] + dy[2]
    gen_small.start()

    @pl.when(h == 0)
    def _():
        for e in range(1, NCOL):
            y_large(1, e).start()

    for e in range(1, NCOL):
        y_large(h, e).start()

    grouped = pan[:, :, :, :, DEPTH:].reshape(4, 16, PAN, 128)
    for q in range(4):
        total = grouped[q, 0]
        for i in range(1, 16):
            total = total + grouped[q, i]
        points[:, 128 * q : 128 * q + 128] = total
    kern = []
    for q in range(4):
        at = slice(128 * q, 128 * q + 128)
        same = jnp.where(lane + 128 * q == sub + PAN * r, f32(nugget_term), f32(0))
        kern.append(matern(own_x - points[0:1, at], own_y - points[1:2, at]) + same)
    gen_small.wait_recv()
    for q in range(4):
        at = slice(128 * q, 128 * q + 128)
        dgat[z, x, core, :, at] = kern[q] - (dy[NCOL - 1, :, at] + dg[:, at])
    second.run()
    work[...] = dgat[...].reshape(B, B)

    for e in range(1, NCOL):
        y_large(1 - h, e).wait_recv()
    gout[...] = u[c, 1 - h] + ybuf[1 - h, 0] + ybuf[1 - h, 1] + ybuf[1 - h, 2]
    gen_large.start()

    linv[...] = jnp.zeros((B, B), f32)

    def combine():
        for e in range(1, NCOL):
            y_large(h, e).wait_recv()
        here = pl.ds(pl.multiple_of((c * 2 + h) * HALF, HALF), HALF)
        mx = jnp.broadcast_to(coords[0:1, here].astype(f32) / GRID, (HALF, HALF)).T
        my = jnp.broadcast_to(coords[1:2, here].astype(f32) / GRID, (HALF, HALF)).T
        isub = lax.broadcasted_iota(jnp.int32, (HALF, 128), 0) + (c * 2 + h) * HALF
        ilane = lax.broadcasted_iota(jnp.int32, (HALF, 128), 1)
        for q in range(4):
            at = slice(128 * q, 128 * q + 128)
            same = (isub < PAN) & (ilane + 128 * q == isub + PAN * r)
            k = matern(mx - points[0:1, at], my - points[1:2, at]) + jnp.where(same, f32(nugget_term), f32(0))
            part = u[c, h, :, at] + ybuf[h, 0, :, at] + ybuf[h, 1, :, at] + ybuf[h, 2, :, at]
            upd[:, at] = k - part

    def settle():
        gen_large.wait_recv()
        upd[...] = upd[...] - gbuf[...]

    slot = c * 2 + h

    def deliver(g):
        return send(
            xs.at[g], xt.at[slot], sx.at[g], rx.at[slot], {"gen": g // NCOL, "col": g % NCOL}
        )

    def solve(v):
        lo, hi = 128 * v, 128 * v + 128
        block = dotf(linv[lo:hi, :hi], upd[:, :hi], ((1,), (1,)))
        for i in range(2):
            g = 2 * v + i
            xs[g] = block[64 * i : 64 * i + 64]

            @pl.when(h * NCOL + c == g)
            def _():
                xt[slot] = xs[g]

            @pl.when(h * NCOL + c != g)
            def _():
                deliver(g).start()

    def step(k, carry):
        for v in range(4):
            @pl.when(k == v)
            def _():
                tile[...] = work[128 * v : 128 * v + 128, 128 * v : 128 * v + 128]
        inverse_factor(tile, inv)
        for v in range(4):
            @pl.when(k == v)
            def _():
                lo, hi = 128 * v, 128 * v + 128
                t = inv[...]
                if v:
                    linv[lo:hi, :lo] = dotf(t, linv[lo:hi, :lo], ((1,), (0,)))
                linv[lo:hi, lo:hi] = t
                if v < 3:
                    p = dotf(t, work[lo:hi, hi:], ((1,), (0,)))
                    work[hi:, hi:] = work[hi:, hi:] - dotf(p, p, ((0,), (0,)))
                    linv[hi:, :hi] = linv[hi:, :hi] - dotf(p, linv[lo:hi, :hi], ((0,), (0,)))
                if v == 1:
                    combine()
                if v == 2:
                    settle()
                    for w in range(3):
                        solve(w)
                if v == 3:
                    solve(3)
        return carry

    lax.fori_loop(0, 4, step, 0)

    for g in range(2 * NCOL):
        @pl.when(h * NCOL + c != g)
        def _():
            theirs = (g % NCOL) * 2 + g // NCOL
            send(xs.at[g], xt.at[theirs], sx.at[g], rx.at[theirs], {"gen": g // NCOL, "col": g % NCOL}).wait_recv()

    for i in range(2 * NCOL):
        out[:, HALF * i : HALF * i + HALF] = xt[i]

    for g in range(2 * NCOL):
        @pl.when(h * NCOL + c != g)
        def _():
            deliver(g).wait_send()
    for e in range(1, NCOL):
        y_small(e).wait_send()
        for s in range(2):
            y_large(s, e).wait_send()
    gen_small.wait_send()
    gen_large.wait_send()
    first.finish()
    second.finish()


def shards(coords, factor):
    dma = pltpu.SemaphoreType.DMA
    vmem = pl.BlockSpec(memory_space=pltpu.VMEM)

    def room(*shape, dtype=jnp.float32):
        return pltpu.VMEM(shape, dtype)

    solved = pl.pallas_call(
        step_kernel,
        out_shape=jax.ShapeDtypeStruct((B // 8, ROWS), jnp.float32),
        in_specs=[vmem, pl.BlockSpec(memory_space=pl.ANY)],
        out_specs=vmem,
        scratch_shapes=[
            room(4, 2, HALF, DEPTH),
            room(NZ, NX, NC, PAN, WIDE),
            room(B, DEPTH, dtype=jnp.bfloat16),
            room(B, DEPTH, dtype=jnp.bfloat16),
            room(4, 2, HALF, B),
            room(NZ, NX, NC, PAN, B),
            room(NCOL, PAN, B),
            room(PAN, B),
            room(2, NCOL - 1, HALF, B),
            room(HALF, B),
            room(HALF, B),
            room(PAN, 128),
            room(PAN, B),
            room(HALF, B),
            room(B, B),
            room(128, 128),
            room(128, 128),
            room(B, B),
            room(2 * NCOL, B // 8, HALF),
            room(2 * NCOL, B // 8, HALF),
            dma((3,)), dma((3,)), dma((3,)), dma((1,)), dma((1,)), dma((2, 3)), dma((2, 3)),
            dma((1,)), dma((1,)), dma((8,)), dma((8,)),
            *gather_sems(), *gather_sems(),
        ],
        compiler_params=pltpu.CompilerParams(
            collective_id=0, has_side_effects=True, vmem_limit_bytes=48 << 20
        ),
        name="panel_step",
    )(coords, factor.reshape(4, 2, HALF, DEPTH))
    return solved.T


def solution(mesh):
    in_specs = (P(None, "row"), P("row", ("gen", "col")))
    out_specs = P("row", ("gen", "col"))
    return jax.shard_map(shards, mesh=mesh, in_specs=in_specs, out_specs=out_specs, check_vma=False)
```

```python
import jax
import jax.numpy as jnp
from jax import lax
from jax.experimental import pallas as pl
from jax.experimental.pallas import tpu as pltpu
from jax.sharding import PartitionSpec as P

B = 512
GRID = 1024
PAN = 8
ROWS = 1024
DEPTH = 1024
HALF = 128
LAG = 2
NZ, NX, NC, NCOL = 8, 4, 2, 4
WIDE = DEPTH + 128

root_three = 1.7320508075688772
length_scale = 0.2
nugget_term = 1.0

HI = lax.Precision.HIGHEST
MESH = pl.DeviceIdType.MESH


def dotf(a, b, dims):
    return lax.dot_general(a, b, (dims, ((), ())), precision=HI, preferred_element_type=jnp.float32)


def matern(delta_x, delta_y):
    scaled = root_three * jnp.sqrt(delta_x * delta_x + delta_y * delta_y) / length_scale
    return (1.0 + scaled) * jnp.exp(-scaled)


def spread(x, k):
    return jnp.broadcast_to(x[k : k + 1], x.shape)


def inverse_factor(tile_ref, out_ref):
    sub = lax.broadcasted_iota(jnp.int32, (8, 128), 0)
    lane = lax.broadcasted_iota(jnp.int32, (8, 128), 1)
    a = [tile_ref[8 * i : 8 * i + 8, :] for i in range(16)]
    t = [jnp.where(lane == sub + 8 * i, jnp.float32(1), jnp.float32(0)) for i in range(16)]
    for b in range(16):
        cols = [jnp.broadcast_to(a[b][:, 8 * b + k : 8 * b + k + 1], (8, 128)) for k in range(8)]
        recip, cross, scale = [], [], jnp.ones((8, 128), jnp.float32)
        for k in range(8):
            pivot = spread(cols[k], k)
            r = 1.0 / pivot
            recip.append(r)
            scale = jnp.where(sub == k, pivot, scale)
            m = jnp.where(sub > k, cols[k] * r, 0.0)
            row = []
            for j in range(k + 1, 8):
                s = spread(cols[j], k)
                row.append(s)
                cols[j] = cols[j] - m * s
            cross.append(row)
            a[b] = a[b] - m * spread(a[b], k)
            t[b] = t[b] - m * spread(t[b], k)
        ua = [spread(a[b], k) for k in range(8)]
        ut = [spread(t[b], k) for k in range(8)]
        out_ref[8 * b : 8 * b + 8, :] = t[b] * lax.rsqrt(scale)
        for i in range(b + 1, 16):
            c = [jnp.broadcast_to(a[i][:, 8 * b + k : 8 * b + k + 1], (8, 128)) for k in range(8)]
            da = dt = None
            for k in range(8):
                m = c[k] * recip[k]
                for j in range(k + 1, 8):
                    c[j] = c[j] - m * cross[k][j - k - 1]
                da = m * ua[k] if da is None else da + m * ua[k]
                dt = m * ut[k] if dt is None else dt + m * ut[k]
            a[i] = a[i] - da
            t[i] = t[i] - dt


def place():
    h, r, c = lax.axis_index("gen"), lax.axis_index("row"), lax.axis_index("col")
    return h, r, c, r // 8, (r // 2) % 4, r % 2


def send(src, dst, send_sem, recv_sem, where):
    return pltpu.make_async_remote_copy(
        src_ref=src, dst_ref=dst, send_sem=send_sem, recv_sem=recv_sem, device_id=where, device_id_type=MESH
    )


class Gather:
    def __init__(self, buf, sz, rz, sx, rx, sc, rc):
        self.buf, self.sz, self.rz, self.sx, self.rx, self.sc, self.rc = buf, sz, rz, sx, rx, sc, rc
        _, self.r, _, self.z, self.x, self.core = place()

    def along_z(self, source, target):
        block = self.buf.at[source, self.x, self.core]
        return send(block, block, self.sz.at[target], self.rz.at[source], {"row": target * 8 + self.x * 2 + self.core})

    def along_x(self, source, e):
        target = (self.x + e) % NX
        block = self.buf.at[source, self.x, self.core]
        return send(block, block, self.sx.at[source, e - 1], self.rx.at[source, self.x],
                    {"row": self.z * 8 + target * 2 + self.core})

    def from_x(self, source, e):
        x = (self.x + e) % NX
        block = self.buf.at[source, x, self.core]
        return send(block, block, self.sx.at[source, 0], self.rx.at[source, x], {"row": self.r + 1 - 2 * self.core})

    def across(self, source, core):
        block = self.buf.at[source, :, core]
        return send(block, block, self.sc.at[source], self.rc.at[source], {"row": self.r + 1 - 2 * self.core})

    def outward(self, visit):
        def ring(k, carry):
            @pl.when(self.z >= k)
            def _():
                visit(self.z - k)

            @pl.when(self.z + k < NZ)
            def _():
                visit(self.z + k)

            return carry

        lax.fori_loop(1, NZ, ring, 0)

    def run(self, middle=None, arrived=None):
        z = self.z
        self.outward(lambda target: self.along_z(z, target).start())

        def spread_x(source):
            for e in range(1, NX):
                self.along_x(source, e).start()

        def forward(source):
            self.along_z(source, z).wait_recv()
            spread_x(source)

        def swap(source):
            for e in range(1, NX):
                self.from_x(source, e).wait_recv()
            self.across(source, self.core).start()

        def arrive(source):
            self.across(source, 1 - self.core).wait_recv()
            if arrived is not None:
                arrived(source)

        spread_x(z)

        def ring(k, carry):
            for act, j in ((forward, k), (swap, k - LAG)):
                @pl.when((j > 0) & (z >= j))
                def _():
                    act(z - j)

                @pl.when((j > 0) & (z + j < NZ))
                def _():
                    act(z + j)

                if act is swap:
                    @pl.when(j == 0)
                    def _():
                        act(z)

            if middle is not None:
                @pl.when(k == NZ - 1)
                def _():
                    middle()

            return carry

        lax.fori_loop(1, NZ + LAG, ring, 0)
        arrive(z)
        self.outward(arrive)

    def finish(self):
        self.outward(lambda target: self.along_z(self.z, target).wait_send())

        def drain(source, carry):
            for e in range(1, NX):
                self.along_x(source, e).wait_send()
            self.across(source, self.core).wait_send()
            return carry

        lax.fori_loop(0, NZ, drain, 0)


def gather_sems():
    dma = pltpu.SemaphoreType.DMA
    return [dma((NZ,)), dma((NZ,)), dma((NZ, NX - 1)), dma((NZ, NX)), dma((NZ,)), dma((NZ,))]


def greet():
    h, r, c, z, x, core = place()
    barrier = pltpu.get_barrier_semaphore()
    peers = [{"row": (z + d) % NZ * 8 + x * 2 + core} for d in range(1, NZ)]
    peers += [{"row": z * 8 + (x + e) % NX * 2 + core} for e in range(1, NX)]
    peers += [{"row": r + 1 - 2 * core}]
    peers += [{"col": (c + e) % NCOL} for e in range(1, NCOL)]
    peers += [{"gen": 1 - h, "col": (c + e) % NCOL} for e in range(NCOL)]
    for peer in peers:
        pl.semaphore_signal(barrier, inc=1, device_id=peer, device_id_type=MESH)
    return lambda: pl.semaphore_wait(barrier, len(peers))


def halves(x):
    high = x.astype(jnp.bfloat16)
    return high, (x - high.astype(jnp.float32)).astype(jnp.bfloat16)


def three(a, b):
    dims = (((1,), (1,)), ((), ()))
    f32 = jnp.float32
    total = lax.dot_general(a[0], b[1], dims, preferred_element_type=f32)
    total += lax.dot_general(a[1], b[0], dims, preferred_element_type=f32)
    return total + lax.dot_general(a[0], b[0], dims, preferred_element_type=f32)


def step_kernel(
    coords, factor, out, place_ref, fv, fhigh, flow, pan, high, low, u, dgat, dall, dsmall, dy, dg, ybuf, gout, gbuf, marks, points, upd,
    work, tile, inv, linv, xs, xt, local, sdy, rdy, sdg, rdg, sy, ry, sg, rg, sx, rx, *sems,
):
    h, r, c, z, x, core = place()
    f32 = jnp.float32
    load = pltpu.make_async_copy(factor, fv, local.at[0])
    rows = pltpu.make_async_copy(factor.at[0, 0, pl.ds(0, PAN), :], pan.at[z, x, core, :, pl.ds(0, DEPTH)], local.at[1])
    where = pltpu.make_async_copy(coords, place_ref, local.at[3])
    where.start()
    rows.start()
    load.start()
    greeted = greet()
    where.wait()

    sub = lax.broadcasted_iota(jnp.int32, (PAN, 128), 0)
    lane = lax.broadcasted_iota(jnp.int32, (PAN, 128), 1)
    start = place_ref[:, :128].astype(f32) / GRID
    mark = jnp.zeros((PAN, 128), f32)
    own_x, own_y = mark, mark
    for j in range(PAN):
        px = jnp.broadcast_to(start[0:1, j : j + 1], (PAN, 128))
        py = jnp.broadcast_to(start[1:2, j : j + 1], (PAN, 128))
        own_x = jnp.where(sub == j, px, own_x)
        own_y = jnp.where(sub == j, py, own_y)
        both = jnp.where(sub == 0, px, jnp.where(sub == 1, py, 0.0))
        mark = jnp.where(lane == (r % 16) * PAN + j, both, mark)
    marks[...] = mark
    tag = pltpu.make_async_copy(marks, pan.at[z, x, core, :, pl.ds(DEPTH, 128)], local.at[2])
    tag.start()
    load.wait()

    def split(i, carry):
        fhigh[i], flow[i] = halves(fv[i])
        return carry

    lax.fori_loop(0, 4, split, 0)
    rows.wait()
    tag.wait()
    greeted()
    first = Gather(pan, *sems[:6])
    second = Gather(dgat, *sems[6:])

    def arrived(source):
        at = pl.ds(pl.multiple_of(source * 64, 64), 64)
        high[at, :], low[at, :] = halves(pan[source, :, :, :, :DEPTH].reshape(64, DEPTH))

    first.run(arrived=arrived)

    def y_small(e):
        return send(dsmall, dy.at[e - 1], sdy.at[e - 1], rdy.at[e - 1], {"col": (c + e) % NCOL})

    def y_large(s, e):
        part = (c + e) % NCOL
        return send(u.at[part, s], ybuf.at[s, e - 1], sy.at[s, e - 1], ry.at[s, e - 1], {"col": part})

    gen_small = send(dy.at[NCOL - 1], dg, sdg.at[0], rdg.at[0], {"gen": 1 - h})
    gen_large = send(gout, gbuf, sg.at[0], rg.at[0], {"gen": 1 - h})

    def tile_of(i):
        return (z // 2 + i) % 4

    def multiply(s):
        a = [part[:, s].reshape(4 * HALF, DEPTH) for part in (fhigh, flow)]
        u[:, s] = three(a, (high[...], low[...])).reshape(4, HALF, B)

    top = [part[0, 0, :16] for part in (fhigh, flow)]
    rows8 = three(top, (high[...], low[...]))[:PAN]
    for q in range(4):
        dall[q] = rows8[:, 128 * q : 128 * q + 128]
    for i in range(3):
        dsmall[i] = dall[tile_of(i)]
    for e in range(1, NCOL):
        y_small(e).start()
    multiply(0)
    for e in range(1, NCOL):
        y_small(e).wait_recv()
    dy[NCOL - 1] = dsmall[...] + dy[0] + dy[1] + dy[2]
    gen_small.start()

    @pl.when(h == 1)
    def _():
        for e in range(1, NCOL):
            y_large(0, e).start()

    multiply(1)

    @pl.when(h == 0)
    def _():
        for e in range(1, NCOL):
            y_large(1, e).start()

    for e in range(1, NCOL):
        y_large(h, e).start()

    grouped = pan[:, :, :, :, DEPTH:].reshape(4, 16, PAN, 128)
    for q in range(4):
        total = grouped[q, 0]
        for i in range(1, 16):
            total = total + grouped[q, i]
        points[q] = total
    kern = []
    for i in range(3):
        marked = points[tile_of(i)]
        same = jnp.where(lane + 128 * tile_of(i) == sub + PAN * r, f32(nugget_term), f32(0))
        kern.append(matern(own_x - marked[0:1], own_y - marked[1:2]) + same)
    here = pl.ds(pl.multiple_of((c * 2 + h) * HALF, HALF), HALF)
    mx = jnp.broadcast_to(place_ref[0:1, here].astype(f32) / GRID, (HALF, HALF)).T
    my = jnp.broadcast_to(place_ref[1:2, here].astype(f32) / GRID, (HALF, HALF)).T
    isub = lax.broadcasted_iota(jnp.int32, (HALF, 128), 0) + (c * 2 + h) * HALF
    ilane = lax.broadcasted_iota(jnp.int32, (HALF, 128), 1)
    for q in range(4):
        at = slice(128 * q, 128 * q + 128)
        same = (isub < PAN) & (ilane + 128 * q == isub + PAN * r)
        k = matern(mx - points[q, 0:1], my - points[q, 1:2]) + jnp.where(same, f32(nugget_term), f32(0))
        upd[:, at] = k
    linv[...] = jnp.zeros((B, B), f32)
    gen_small.wait_recv()
    for i in range(3):
        dgat[z, x, core, i] = kern[i] - (dy[NCOL - 1, i] + dg[i])

    def pass_on():
        for e in range(1, NCOL):
            y_large(1 - h, e).wait_recv()
        gout[...] = u[c, 1 - h] + ybuf[1 - h, 0] + ybuf[1 - h, 1] + ybuf[1 - h, 2]
        gen_large.start()

    second.run(middle=pass_on)
    for t, i in ((0, 0), (0, 1), (0, 2), (1, 0), (1, 1), (1, 2), (2, 0), (2, 1), (3, 0), (3, 1)):
        block = dgat[2 * t : 2 * t + 2, :, :, i].reshape(128, 128)
        if t + i == 4:
            block, row, col = block.T, 0, 3
        else:
            row, col = t, t + i
        work[128 * row : 128 * row + 128, 128 * col : 128 * col + 128] = block

    def combine():
        for e in range(1, NCOL):
            y_large(h, e).wait_recv()
        for q in range(4):
            at = slice(128 * q, 128 * q + 128)
            part = u[c, h, :, at] + ybuf[h, 0, :, at] + ybuf[h, 1, :, at] + ybuf[h, 2, :, at]
            upd[:, at] = upd[:, at] - part

    def settle():
        gen_large.wait_recv()
        upd[...] = upd[...] - gbuf[...]

    slot = c * 2 + h

    def deliver(g):
        return send(
            xs.at[g], xt.at[slot], sx.at[g], rx.at[slot], {"gen": g // NCOL, "col": g % NCOL}
        )

    def solve(v):
        lo, hi = 128 * v, 128 * v + 128
        block = dotf(linv[lo:hi, :hi], upd[:, :hi], ((1,), (1,)))
        for i in range(2):
            g = 2 * v + i
            xs[g] = block[64 * i : 64 * i + 64]

            @pl.when(h * NCOL + c == g)
            def _():
                xt[slot] = xs[g]

            @pl.when(h * NCOL + c != g)
            def _():
                deliver(g).start()

    def step(k, carry):
        for v in range(4):
            @pl.when(k == v)
            def _():
                tile[...] = work[128 * v : 128 * v + 128, 128 * v : 128 * v + 128]
        inverse_factor(tile, inv)
        for v in range(4):
            @pl.when(k == v)
            def _():
                lo, hi = 128 * v, 128 * v + 128
                t = inv[...]
                if v:
                    linv[lo:hi, :lo] = dotf(t, linv[lo:hi, :lo], ((1,), (0,)))
                linv[lo:hi, lo:hi] = t
                if v < 3:
                    p = dotf(t, work[lo:hi, hi:], ((1,), (0,)))
                    for w in range(v + 1, 4):
                        at = slice(128 * w, 128 * w + 128)
                        left = slice(128 * w - hi, 128 * w + 128 - hi)
                        work[at, 128 * w :] = work[at, 128 * w :] - dotf(p[:, left], p[:, 128 * w - hi :], ((0,), (0,)))
                    linv[hi:, :hi] = linv[hi:, :hi] - dotf(p, linv[lo:hi, :hi], ((0,), (0,)))
                if v == 1:
                    combine()
                if v == 2:
                    settle()
                    for w in range(3):
                        solve(w)
                if v == 3:
                    solve(3)
        return carry

    lax.fori_loop(0, 4, step, 0)

    for g in range(2 * NCOL):
        @pl.when(h * NCOL + c != g)
        def _():
            theirs = (g % NCOL) * 2 + g // NCOL
            send(xs.at[g], xt.at[theirs], sx.at[g], rx.at[theirs], {"gen": g // NCOL, "col": g % NCOL}).wait_recv()

    for i in range(2 * NCOL):
        out[:, HALF * i : HALF * i + HALF] = xt[i]

    for g in range(2 * NCOL):
        @pl.when(h * NCOL + c != g)
        def _():
            deliver(g).wait_send()
    for e in range(1, NCOL):
        y_small(e).wait_send()
        for s in range(2):
            y_large(s, e).wait_send()
    gen_small.wait_send()
    gen_large.wait_send()
    first.finish()
    second.finish()


def shards(coords, factor):
    dma = pltpu.SemaphoreType.DMA
    vmem = pl.BlockSpec(memory_space=pltpu.VMEM)

    def room(*shape, dtype=jnp.float32):
        return pltpu.VMEM(shape, dtype)

    solved = pl.pallas_call(
        step_kernel,
        out_shape=jax.ShapeDtypeStruct((B // 8, ROWS), jnp.float32),
        in_specs=[pl.BlockSpec(memory_space=pltpu.HBM)] * 2,
        out_specs=vmem,
        scratch_shapes=[
            room(2, ROWS, dtype=jnp.int32),
            room(4, 2, HALF, DEPTH),
            room(4, 2, HALF, DEPTH, dtype=jnp.bfloat16),
            room(4, 2, HALF, DEPTH, dtype=jnp.bfloat16),
            room(NZ, NX, NC, PAN, WIDE),
            room(B, DEPTH, dtype=jnp.bfloat16),
            room(B, DEPTH, dtype=jnp.bfloat16),
            room(4, 2, HALF, B),
            room(NZ, NX, NC, 3, PAN, 128),
            room(4, PAN, 128),
            room(3, PAN, 128),
            room(NCOL, 3, PAN, 128),
            room(3, PAN, 128),
            room(2, NCOL - 1, HALF, B),
            room(HALF, B),
            room(HALF, B),
            room(PAN, 128),
            room(4, PAN, 128),
            room(HALF, B),
            room(B, B),
            room(128, 128),
            room(128, 128),
            room(B, B),
            room(2 * NCOL, B // 8, HALF),
            room(2 * NCOL, B // 8, HALF),
            dma((4,)), dma((3,)), dma((3,)), dma((1,)), dma((1,)), dma((2, 3)), dma((2, 3)),
            dma((1,)), dma((1,)), dma((8,)), dma((8,)),
            *gather_sems(), *gather_sems(),
        ],
        compiler_params=pltpu.CompilerParams(
            collective_id=0, has_side_effects=True, vmem_limit_bytes=60 << 20
        ),
        name="panel_step",
    )(coords, factor.reshape(4, 2, HALF, DEPTH))
    return solved.T


def solution(mesh):
    in_specs = (P(None, "row"), P("row", ("gen", "col")))
    out_specs = P("row", ("gen", "col"))
    return jax.shard_map(shards, mesh=mesh, in_specs=in_specs, out_specs=out_specs, check_vma=False)
```

```python
import jax
import jax.numpy as jnp
from jax import lax
from jax.experimental import pallas as pl
from jax.experimental.pallas import tpu as pltpu
from jax.sharding import PartitionSpec as P

B = 512
GRID = 1024
PAN = 8
ROWS = 1024
DEPTH = 1024
HALF = 128
LAG = 2
NZ, NX, NC, NCOL = 8, 4, 2, 4
WIDE = DEPTH + 128

root_three = 1.7320508075688772
length_scale = 0.2
nugget_term = 1.0

HI = lax.Precision.HIGHEST
MESH = pl.DeviceIdType.MESH


def dotf(a, b, dims):
    return lax.dot_general(a, b, (dims, ((), ())), precision=HI, preferred_element_type=jnp.float32)


def matern(delta_x, delta_y):
    scaled = root_three * jnp.sqrt(delta_x * delta_x + delta_y * delta_y) / length_scale
    return (1.0 + scaled) * jnp.exp(-scaled)


def spread(x, k):
    return jnp.broadcast_to(x[k : k + 1], x.shape)


def inverse_factor(tile_ref, out_ref):
    sub = lax.broadcasted_iota(jnp.int32, (8, 128), 0)
    lane = lax.broadcasted_iota(jnp.int32, (8, 128), 1)
    a = [tile_ref[8 * i : 8 * i + 8, :] for i in range(16)]
    t = [jnp.where(lane == sub + 8 * i, jnp.float32(1), jnp.float32(0)) for i in range(16)]
    for b in range(16):
        cols = [jnp.broadcast_to(a[b][:, 8 * b + k : 8 * b + k + 1], (8, 128)) for k in range(8)]
        recip, cross, scale = [], [], jnp.ones((8, 128), jnp.float32)
        for k in range(8):
            pivot = spread(cols[k], k)
            r = 1.0 / pivot
            recip.append(r)
            scale = jnp.where(sub == k, pivot, scale)
            m = jnp.where(sub > k, cols[k] * r, 0.0)
            row = []
            for j in range(k + 1, 8):
                s = spread(cols[j], k)
                row.append(s)
                cols[j] = cols[j] - m * s
            cross.append(row)
            a[b] = a[b] - m * spread(a[b], k)
            t[b] = t[b] - m * spread(t[b], k)
        ua = [spread(a[b], k) for k in range(8)]
        ut = [spread(t[b], k) for k in range(8)]
        out_ref[8 * b : 8 * b + 8, :] = t[b] * lax.rsqrt(scale)
        inverse_pivots = jnp.ones((8, 128), jnp.float32)
        for k in range(8):
            inverse_pivots = jnp.where(sub == k, recip[k], inverse_pivots)
        scaled = a[b] * inverse_pivots
        for i in range(b + 1, min(b + 1 + 2, 16)):
            c = [jnp.broadcast_to(a[i][:, 8 * b + k : 8 * b + k + 1], (8, 128)) for k in range(8)]
            da = dt = None
            for k in range(8):
                m = c[k] * recip[k]
                for j in range(k + 1, 8):
                    c[j] = c[j] - m * cross[k][j - k - 1]
                da = m * ua[k] if da is None else da + m * ua[k]
                dt = m * ut[k] if dt is None else dt + m * ut[k]
            a[i] = a[i] - da
            t[i] = t[i] - dt
        if b + 1 + 2 < 16:
            hi = scaled.astype(jnp.bfloat16).astype(jnp.float32); r1 = scaled - hi
            mi = r1.astype(jnp.bfloat16).astype(jnp.float32); lo = r1 - mi
            both = jnp.concatenate([a[b], t[b]], axis=1)
            bh = both.astype(jnp.bfloat16).astype(jnp.float32); r2 = both - bh
            bm = r2.astype(jnp.bfloat16).astype(jnp.float32); bl = r2 - bm
            lhs = jnp.concatenate([hi, hi, mi, hi, lo, mi, hi, hi], axis=0).astype(jnp.bfloat16)
            rhs = jnp.concatenate([bh, bm, bh, bl, bh, bm, 0 * bh, 0 * bh], axis=0).astype(jnp.bfloat16)
            delta = lax.dot_general(lhs, rhs, (((0,), (0,)), ((), ())), preferred_element_type=jnp.float32)
            for i in range(b + 1 + 2, 16):
                a[i] = a[i] - delta[8 * i : 8 * i + 8, :128]
                t[i] = t[i] - delta[8 * i : 8 * i + 8, 128:]
def place():
    h, r, c = lax.axis_index("gen"), lax.axis_index("row"), lax.axis_index("col")
    return h, r, c, r // 8, (r // 2) % 4, r % 2


def send(src, dst, send_sem, recv_sem, where):
    return pltpu.make_async_remote_copy(
        src_ref=src, dst_ref=dst, send_sem=send_sem, recv_sem=recv_sem, device_id=where, device_id_type=MESH
    )


class Gather:
    def __init__(self, buf, sx, rx, sc, rc):
        self.buf, self.sx, self.rx, self.sc, self.rc = buf, sx, rx, sc, rc
        _, self.r, _, self.z, self.x, self.core = place()

    def along_x(self, source, e):
        target = (self.x + e) % NX
        block = self.buf.at[source, self.x, self.core]
        return send(block, block, self.sx.at[source, e - 1], self.rx.at[source, self.x],
                    {"row": self.z * 8 + target * 2 + self.core})

    def from_x(self, source, e):
        x = (self.x + e) % NX
        block = self.buf.at[source, x, self.core]
        return send(block, block, self.sx.at[source, 0], self.rx.at[source, x], {"row": self.r + 1 - 2 * self.core})

    def across(self, source, core):
        block = self.buf.at[source, :, core]
        return send(block, block, self.sc.at[source], self.rc.at[source], {"row": self.r + 1 - 2 * self.core})

    def run(self, away, fetch, aside, arrived=None):
        z = self.z

        def forward(source):
            fetch(source)
            for e in range(1, NX):
                self.along_x(source, e).start()

        def swap(source):
            for e in range(1, NX):
                self.from_x(source, e).wait_recv()
            self.across(source, self.core).start()

        def arrive(source):
            self.across(source, 1 - self.core).wait_recv()
            if arrived is not None:
                arrived(source)

        def visit(act, k):
            d = away(k)
            inside = (k >= 0) & (k < NZ)

            @pl.when(inside & (z >= d))
            def _():
                act(z - d)

            @pl.when(inside & (d > 0) & (z + d < NZ))
            def _():
                act(z + d)

        def ring(k, carry):
            visit(forward, k)
            aside(k)
            visit(swap, k - LAG)
            return carry

        def last(k, carry):
            visit(arrive, k)
            return carry

        lax.fori_loop(0, NZ + LAG, ring, 0)
        lax.fori_loop(0, NZ, last, 0)

    def finish(self):
        def drain(source, carry):
            for e in range(1, NX):
                self.along_x(source, e).wait_send()
            self.across(source, self.core).wait_send()
            return carry

        lax.fori_loop(0, NZ, drain, 0)


def gather_sems():
    dma = pltpu.SemaphoreType.DMA
    return [dma((NZ, NX - 1)), dma((NZ, NX)), dma((NZ,)), dma((NZ,))]


def greet():
    h, r, c, z, x, core = place()
    barrier = pltpu.get_barrier_semaphore()
    peers = [{"row": (z + d) % NZ * 8 + x * 2 + core} for d in range(1, NZ)]
    peers += [{"row": z * 8 + (x + e) % NX * 2 + core} for e in range(1, NX)]
    peers += [{"row": r + 1 - 2 * core}]
    peers += [{"col": (c + e) % NCOL} for e in range(1, NCOL)]
    peers += [{"gen": 1 - h, "col": (c + e) % NCOL} for e in range(NCOL)]
    peers += [{"gen": 1 - h, "row": (z + d) % NZ * 8 + x * 2 + core} for d in range(1, NZ)]
    for peer in peers:
        pl.semaphore_signal(barrier, inc=1, device_id=peer, device_id_type=MESH)
    return lambda: pl.semaphore_wait(barrier, len(peers))


def halves(x):
    high = x.astype(jnp.bfloat16)
    return high, (x - high.astype(jnp.float32)).astype(jnp.bfloat16)


def three(a, b):
    dims = (((1,), (1,)), ((), ()))
    f32 = jnp.float32
    total = lax.dot_general(a[0], b[1], dims, preferred_element_type=f32)
    total += lax.dot_general(a[1], b[0], dims, preferred_element_type=f32)
    return total + lax.dot_general(a[0], b[0], dims, preferred_element_type=f32)


def step_kernel(
    coords, factor, out, place_ref, fv, fhigh, flow, pan, high, low, u, dgat, dall, dsmall, dy, dpart, ybuf, gout, gbuf, points, upd,
    work, tile, inv, linv, xs, xt, local, sz, rz, sdy, rdy, sdg, rdg, sy, ry, sg, rg, sx, rx, *sems,
):
    h, r, c, z, x, core = place()
    f32 = jnp.float32
    load = pltpu.make_async_copy(factor, fv, local.at[0])
    rows = pltpu.make_async_copy(factor.at[0, 0, pl.ds(0, PAN), :], pan.at[z, x, core, :, pl.ds(0, DEPTH)], local.at[1])
    where = pltpu.make_async_copy(coords, place_ref, local.at[3])
    where.start()
    rows.start()
    load.start()
    greeted = greet()
    where.wait()

    sub = lax.broadcasted_iota(jnp.int32, (PAN, 128), 0)
    lane = lax.broadcasted_iota(jnp.int32, (PAN, 128), 1)
    start = place_ref[:, :128].astype(f32) / GRID
    mark = jnp.zeros((PAN, 128), f32)
    own_x, own_y = mark, mark
    for j in range(PAN):
        px = jnp.broadcast_to(start[0:1, j : j + 1], (PAN, 128))
        py = jnp.broadcast_to(start[1:2, j : j + 1], (PAN, 128))
        own_x = jnp.where(sub == j, px, own_x)
        own_y = jnp.where(sub == j, py, own_y)
        both = jnp.where(sub == 0, px, jnp.where(sub == 1, py, 0.0))
        mark = jnp.where(lane == (r % 16) * PAN + j, both, mark)
    pan[z, x, core, :, DEPTH:] = mark
    rows.wait()
    greeted()

    first = Gather(pan, *sems[:4])
    second = Gather(dgat, *sems[4:])

    def panel_copy(source, target):
        block = pan.at[source, x, core]
        return send(block, block, sz.at[target], rz.at[source], {"row": target * 8 + x * 2 + core})

    def panel_each(act):
        def ring(k, carry):
            @pl.when(z >= k)
            def _():
                act(panel_copy(z, z - k))

            @pl.when(z + k < NZ)
            def _():
                act(panel_copy(z, z + k))

            return carry

        lax.fori_loop(1, NZ, ring, 0)

    panel_each(lambda copy: copy.start())
    load.wait()

    def panel_fetch(source):
        @pl.when(source != z)
        def _():
            panel_copy(source, z).wait_recv()

    def split(k):
        @pl.when(k < 8)
        def _():
            fhigh[k // 2, k % 2], flow[k // 2, k % 2] = halves(fv[k // 2, k % 2])

    def arrived(source):
        at = pl.ds(pl.multiple_of(source * 64, 64), 64)
        high[at, :], low[at, :] = halves(pan[source, :, :, :, :DEPTH].reshape(64, DEPTH))

    first.run(lambda k: k, panel_fetch, split, arrived)

    def y_small(e):
        return send(dsmall, dy.at[e - 1], sdy.at[e - 1], rdy.at[e - 1], {"col": (c + e) % NCOL})

    def y_large(s, e):
        part = (c + e) % NCOL
        return send(u.at[part, s], ybuf.at[s, e - 1], sy.at[s, e - 1], ry.at[s, e - 1], {"col": part})

    ring_place = h * NZ + z

    def part_copy(source, target):
        block = dpart.at[source]
        return send(block, block, sdg.at[target], rdg.at[source],
                    {"gen": target // NZ, "row": target % NZ * 8 + x * 2 + core})

    def part_each(act):
        def ring(k, carry):
            act(part_copy(ring_place, (ring_place + k) % (2 * NZ)))

            @pl.when(k < NZ)
            def _():
                act(part_copy(ring_place, (ring_place + 2 * NZ - k) % (2 * NZ)))

            return carry

        lax.fori_loop(1, NZ + 1, ring, 0)

    def part_fetch(source):
        for g in range(2):
            @pl.when(ring_place != g * NZ + source)
            def _():
                part_copy(g * NZ + source, ring_place).wait_recv()

        dgat[source, x, core] = dpart[source] + dpart[NZ + source]

    gen_large = send(gout, gbuf, sg.at[0], rg.at[0], {"gen": 1 - h})

    def tile_of(i):
        return (z // 2 + i) % 4

    def multiply(s):
        a = [part[:, s].reshape(4 * HALF, DEPTH) for part in (fhigh, flow)]
        u[:, s] = three(a, (high[...], low[...])).reshape(4, HALF, B)

    top = [part[0, 0, :16] for part in (fhigh, flow)]
    rows8 = three(top, (high[...], low[...]))[:PAN]
    for q in range(4):
        dall[q] = rows8[:, 128 * q : 128 * q + 128]
    for i in range(3):
        dsmall[i] = dall[tile_of(i)]
    for e in range(1, NCOL):
        y_small(e).start()
    grouped = pan[:, :, :, :, DEPTH:].reshape(4, 16, PAN, 128)
    for q in range(4):
        total = grouped[q, 0]
        for i in range(1, 16):
            total = total + grouped[q, i]
        points[q] = total
    kern = []
    for i in range(3):
        marked = points[tile_of(i)]
        same = jnp.where(lane + 128 * tile_of(i) == sub + PAN * r, f32(nugget_term), f32(0))
        kern.append(matern(own_x - marked[0:1], own_y - marked[1:2]) + same)
    multiply(0)
    for e in range(1, NCOL):
        y_small(e).wait_recv()
    for i in range(3):
        total = dsmall[i] + dy[0, i] + dy[1, i] + dy[2, i]
        dpart[ring_place, i] = jnp.where(h == 0, kern[i], 0.0) - total
    part_each(lambda copy: copy.start())

    @pl.when(h == 1)
    def _():
        for e in range(1, NCOL):
            y_large(0, e).start()

    multiply(1)

    @pl.when(h == 0)
    def _():
        for e in range(1, NCOL):
            y_large(1, e).start()

    for e in range(1, NCOL):
        y_large(h, e).start()

    here = pl.ds(pl.multiple_of((c * 2 + h) * HALF, HALF), HALF)
    mx = jnp.broadcast_to(place_ref[0:1, here].astype(f32) / GRID, (HALF, HALF)).T
    my = jnp.broadcast_to(place_ref[1:2, here].astype(f32) / GRID, (HALF, HALF)).T
    isub = lax.broadcasted_iota(jnp.int32, (HALF, 128), 0) + (c * 2 + h) * HALF
    ilane = lax.broadcasted_iota(jnp.int32, (HALF, 128), 1)
    for q in range(4):
        at = slice(128 * q, 128 * q + 128)
        same = (isub < PAN) & (ilane + 128 * q == isub + PAN * r)
        k = matern(mx - points[q, 0:1], my - points[q, 1:2]) + jnp.where(same, f32(nugget_term), f32(0))
        upd[:, at] = k
    linv[...] = jnp.zeros((B, B), f32)
    def pass_on(k):
        @pl.when(k == NZ - 1)
        def _():
            for e in range(1, NCOL):
                y_large(1 - h, e).wait_recv()
            gout[...] = u[c, 1 - h] + ybuf[1 - h, 0] + ybuf[1 - h, 1] + ybuf[1 - h, 2]
            gen_large.start()

    second.run(lambda k: NZ // 2 + ((k + 1) // 2) * (1 - 2 * (k % 2)), part_fetch, pass_on)
    for t, i in ((0, 0), (0, 1), (0, 2), (1, 0), (1, 1), (1, 2), (2, 0), (2, 1), (3, 0), (3, 1)):
        block = dgat[2 * t : 2 * t + 2, :, :, i].reshape(128, 128)
        if t + i == 4:
            block, row, col = block.T, 0, 3
        else:
            row, col = t, t + i
        work[128 * row : 128 * row + 128, 128 * col : 128 * col + 128] = block

    def combine():
        for e in range(1, NCOL):
            y_large(h, e).wait_recv()
        for q in range(4):
            at = slice(128 * q, 128 * q + 128)
            part = u[c, h, :, at] + ybuf[h, 0, :, at] + ybuf[h, 1, :, at] + ybuf[h, 2, :, at]
            upd[:, at] = upd[:, at] - part

    def settle():
        gen_large.wait_recv()
        upd[...] = upd[...] - gbuf[...]

    slot = c * 2 + h

    def deliver(g):
        return send(
            xs.at[g], xt.at[slot], sx.at[g], rx.at[slot], {"gen": g // NCOL, "col": g % NCOL}
        )

    def solve(v):
        lo, hi = 128 * v, 128 * v + 128
        block = dotf(linv[lo:hi, :hi], upd[:, :hi], ((1,), (1,)))
        for i in range(2):
            g = 2 * v + i
            xs[g] = block[64 * i : 64 * i + 64]

            @pl.when(h * NCOL + c == g)
            def _():
                xt[slot] = xs[g]

            @pl.when(h * NCOL + c != g)
            def _():
                deliver(g).start()

    def step(k, carry):
        for v in range(4):
            @pl.when(k == v)
            def _():
                tile[...] = work[128 * v : 128 * v + 128, 128 * v : 128 * v + 128]
        inverse_factor(tile, inv)
        for v in range(4):
            @pl.when(k == v)
            def _():
                lo, hi = 128 * v, 128 * v + 128
                t = inv[...]
                if v:
                    linv[lo:hi, :lo] = dotf(t, linv[lo:hi, :lo], ((1,), (0,)))
                linv[lo:hi, lo:hi] = t
                if v < 3:
                    p = dotf(t, work[lo:hi, hi:], ((1,), (0,)))
                    for w in range(v + 1, 4):
                        at = slice(128 * w, 128 * w + 128)
                        left = slice(128 * w - hi, 128 * w + 128 - hi)
                        work[at, 128 * w :] = work[at, 128 * w :] - dotf(p[:, left], p[:, 128 * w - hi :], ((0,), (0,)))
                    linv[hi:, :hi] = linv[hi:, :hi] - dotf(p, linv[lo:hi, :hi], ((0,), (0,)))
                if v == 1:
                    combine()
                if v == 2:
                    settle()
                    for w in range(3):
                        solve(w)
                if v == 3:
                    solve(3)
        return carry

    lax.fori_loop(0, 4, step, 0)

    for g in range(2 * NCOL):
        @pl.when(h * NCOL + c != g)
        def _():
            theirs = (g % NCOL) * 2 + g // NCOL
            send(xs.at[g], xt.at[theirs], sx.at[g], rx.at[theirs], {"gen": g // NCOL, "col": g % NCOL}).wait_recv()

    for i in range(2 * NCOL):
        out[:, HALF * i : HALF * i + HALF] = xt[i]

    for g in range(2 * NCOL):
        @pl.when(h * NCOL + c != g)
        def _():
            deliver(g).wait_send()
    for e in range(1, NCOL):
        y_small(e).wait_send()
        for s in range(2):
            y_large(s, e).wait_send()
    part_each(lambda copy: copy.wait_send())
    panel_each(lambda copy: copy.wait_send())
    gen_large.wait_send()
    first.finish()
    second.finish()


def shards(coords, factor):
    dma = pltpu.SemaphoreType.DMA
    vmem = pl.BlockSpec(memory_space=pltpu.VMEM)

    def room(*shape, dtype=jnp.float32):
        return pltpu.VMEM(shape, dtype)

    solved = pl.pallas_call(
        step_kernel,
        out_shape=jax.ShapeDtypeStruct((B // 8, ROWS), jnp.float32),
        in_specs=[pl.BlockSpec(memory_space=pltpu.HBM)] * 2,
        out_specs=vmem,
        scratch_shapes=[
            room(2, ROWS, dtype=jnp.int32),
            room(4, 2, HALF, DEPTH),
            room(4, 2, HALF, DEPTH, dtype=jnp.bfloat16),
            room(4, 2, HALF, DEPTH, dtype=jnp.bfloat16),
            room(NZ, NX, NC, PAN, WIDE),
            room(B, DEPTH, dtype=jnp.bfloat16),
            room(B, DEPTH, dtype=jnp.bfloat16),
            room(4, 2, HALF, B),
            room(NZ, NX, NC, 3, PAN, 128),
            room(4, PAN, 128),
            room(3, PAN, 128),
            room(NCOL - 1, 3, PAN, 128),
            room(2 * NZ, 3, PAN, 128),
            room(2, NCOL - 1, HALF, B),
            room(HALF, B),
            room(HALF, B),
            room(4, PAN, 128),
            room(HALF, B),
            room(B, B),
            room(128, 128),
            room(128, 128),
            room(B, B),
            room(2 * NCOL, B // 8, HALF),
            room(2 * NCOL, B // 8, HALF),
            dma((4,)), dma((NZ,)), dma((NZ,)), dma((3,)), dma((3,)), dma((2 * NZ,)), dma((2 * NZ,)), dma((2, 3)), dma((2, 3)),
            dma((1,)), dma((1,)), dma((8,)), dma((8,)),
            *gather_sems(), *gather_sems(),
        ],
        compiler_params=pltpu.CompilerParams(
            collective_id=0, has_side_effects=True, vmem_limit_bytes=60 << 20
        ),
        name="panel_step",
    )(coords, factor.reshape(4, 2, HALF, DEPTH))
    return solved.T


def solution(mesh):
    in_specs = (P(None, "row"), P("row", ("gen", "col")))
    out_specs = P("row", ("gen", "col"))
    return jax.shard_map(shards, mesh=mesh, in_specs=in_specs, out_specs=out_specs, check_vma=False)
```

```python
import jax
import jax.numpy as jnp
from jax import lax
from jax.experimental import pallas as pl
from jax.experimental.pallas import tpu as pltpu
from jax.sharding import PartitionSpec as P

B = 512
GRID = 1024
PAN = 8
ROWS = 1024
DEPTH = 1024
HALF = 128
LAG = 2
NZ, NX, NC, NCOL = 8, 4, 2, 4
WIDE = DEPTH + 128

root_three = 1.7320508075688772
length_scale = 0.2
nugget_term = 1.0

HI = lax.Precision.HIGHEST
MESH = pl.DeviceIdType.MESH


def dotf(a, b, dims):
    return lax.dot_general(a, b, (dims, ((), ())), precision=HI, preferred_element_type=jnp.float32)


def matern(delta_x, delta_y):
    scaled = root_three * jnp.sqrt(delta_x * delta_x + delta_y * delta_y) / length_scale
    return (1.0 + scaled) * jnp.exp(-scaled)


def spread(x, k):
    return jnp.broadcast_to(x[k : k + 1], x.shape)


def inverse_factor(tile_ref, out_ref):
    sub = lax.broadcasted_iota(jnp.int32, (8, 128), 0)
    lane = lax.broadcasted_iota(jnp.int32, (8, 128), 1)
    a = [tile_ref[8 * i : 8 * i + 8, :] for i in range(16)]
    t = [jnp.where(lane == sub + 8 * i, jnp.float32(1), jnp.float32(0)) for i in range(16)]
    for b in range(16):
        cols = [jnp.broadcast_to(a[b][:, 8 * b + k : 8 * b + k + 1], (8, 128)) for k in range(8)]
        recip, cross, scale = [], [], jnp.ones((8, 128), jnp.float32)
        for k in range(8):
            pivot = spread(cols[k], k)
            r = 1.0 / pivot
            recip.append(r)
            scale = jnp.where(sub == k, pivot, scale)
            m = jnp.where(sub > k, cols[k] * r, 0.0)
            row = []
            for j in range(k + 1, 8):
                s = spread(cols[j], k)
                row.append(s)
                cols[j] = cols[j] - m * s
            cross.append(row)
            a[b] = a[b] - m * spread(a[b], k)
            t[b] = t[b] - m * spread(t[b], k)
        ua = [spread(a[b], k) for k in range(8)]
        ut = [spread(t[b], k) for k in range(8)]
        out_ref[8 * b : 8 * b + 8, :] = t[b] * lax.rsqrt(scale)
        inverse_pivots = jnp.ones((8, 128), jnp.float32)
        for k in range(8):
            inverse_pivots = jnp.where(sub == k, recip[k], inverse_pivots)
        scaled = a[b] * inverse_pivots
        for i in range(b + 1, min(b + 1 + 2, 16)):
            c = [jnp.broadcast_to(a[i][:, 8 * b + k : 8 * b + k + 1], (8, 128)) for k in range(8)]
            da = dt = None
            for k in range(8):
                m = c[k] * recip[k]
                for j in range(k + 1, 8):
                    c[j] = c[j] - m * cross[k][j - k - 1]
                da = m * ua[k] if da is None else da + m * ua[k]
                dt = m * ut[k] if dt is None else dt + m * ut[k]
            a[i] = a[i] - da
            t[i] = t[i] - dt
        if b + 1 + 2 < 16:
            hi = scaled.astype(jnp.bfloat16).astype(jnp.float32); r1 = scaled - hi
            mi = r1.astype(jnp.bfloat16).astype(jnp.float32); lo = r1 - mi
            both = jnp.concatenate([a[b], t[b]], axis=1)
            bh = both.astype(jnp.bfloat16).astype(jnp.float32); r2 = both - bh
            bm = r2.astype(jnp.bfloat16).astype(jnp.float32); bl = r2 - bm
            lhs = jnp.concatenate([hi, hi, mi, hi, lo, mi, hi, hi], axis=0).astype(jnp.bfloat16)
            rhs = jnp.concatenate([bh, bm, bh, bl, bh, bm, 0 * bh, 0 * bh], axis=0).astype(jnp.bfloat16)
            delta = lax.dot_general(lhs, rhs, (((0,), (0,)), ((), ())), preferred_element_type=jnp.float32)
            for i in range(b + 1 + 2, 16):
                a[i] = a[i] - delta[8 * i : 8 * i + 8, :128]
                t[i] = t[i] - delta[8 * i : 8 * i + 8, 128:]
def place():
    h, r, c = lax.axis_index("gen"), lax.axis_index("row"), lax.axis_index("col")
    return h, r, c, r // 8, (r // 2) % 4, r % 2


def send(src, dst, send_sem, recv_sem, where):
    return pltpu.make_async_remote_copy(
        src_ref=src, dst_ref=dst, send_sem=send_sem, recv_sem=recv_sem, device_id=where, device_id_type=MESH
    )


class Gather:
    def __init__(self, buf, sx, rx, sc, rc):
        self.buf, self.sx, self.rx, self.sc, self.rc = buf, sx, rx, sc, rc
        _, self.r, _, self.z, self.x, self.core = place()

    def along_x(self, source, e):
        target = (self.x + e) % NX
        block = self.buf.at[source, self.x, self.core]
        return send(block, block, self.sx.at[source, e - 1], self.rx.at[source, self.x],
                    {"row": self.z * 8 + target * 2 + self.core})

    def from_x(self, source, e):
        x = (self.x + e) % NX
        block = self.buf.at[source, x, self.core]
        return send(block, block, self.sx.at[source, 0], self.rx.at[source, x], {"row": self.r + 1 - 2 * self.core})

    def across(self, source, core):
        block = self.buf.at[source, :, core]
        return send(block, block, self.sc.at[source], self.rc.at[source], {"row": self.r + 1 - 2 * self.core})

    def run(self, away, fetch, aside, arrived=None):
        z = self.z

        def forward(source):
            fetch(source)
            for e in range(1, NX):
                self.along_x(source, e).start()

        def swap(source):
            for e in range(1, NX):
                self.from_x(source, e).wait_recv()
            self.across(source, self.core).start()

        def arrive(source):
            self.across(source, 1 - self.core).wait_recv()
            if arrived is not None:
                arrived(source)

        def visit(act, k):
            d = away(k)
            inside = (k >= 0) & (k < NZ)

            @pl.when(inside & (z >= d))
            def _():
                act(z - d)

            @pl.when(inside & (d > 0) & (z + d < NZ))
            def _():
                act(z + d)

        def ring(k, carry):
            visit(forward, k)
            aside(k)
            visit(swap, k - LAG)
            return carry

        def last(k, carry):
            visit(arrive, k)
            return carry

        lax.fori_loop(0, NZ + LAG, ring, 0)
        lax.fori_loop(0, NZ, last, 0)

    def finish(self):
        def drain(source, carry):
            for e in range(1, NX):
                self.along_x(source, e).wait_send()
            self.across(source, self.core).wait_send()
            return carry

        lax.fori_loop(0, NZ, drain, 0)


def gather_sems():
    dma = pltpu.SemaphoreType.DMA
    return [dma((NZ, NX - 1)), dma((NZ, NX)), dma((NZ,)), dma((NZ,))]


def greet():
    h, r, c, z, x, core = place()
    barrier = pltpu.get_barrier_semaphore()
    peers = [{"row": (z + d) % NZ * 8 + x * 2 + core} for d in range(1, NZ)]
    peers += [{"row": z * 8 + (x + e) % NX * 2 + core} for e in range(1, NX)]
    peers += [{"row": r + 1 - 2 * core}]
    peers += [{"col": (c + e) % NCOL} for e in range(1, NCOL)]
    peers += [{"gen": 1 - h, "col": (c + e) % NCOL} for e in range(NCOL)]
    peers += [{"gen": 1 - h, "row": (z + d) % NZ * 8 + x * 2 + core} for d in range(1, NZ)]
    for peer in peers:
        pl.semaphore_signal(barrier, inc=1, device_id=peer, device_id_type=MESH)
    return lambda: pl.semaphore_wait(barrier, len(peers))


def halves(x):
    high = x.astype(jnp.bfloat16)
    return high, (x - high.astype(jnp.float32)).astype(jnp.bfloat16)


def three(a, b):
    dims = (((1,), (1,)), ((), ()))
    f32 = jnp.float32
    total = lax.dot_general(a[0], b[1], dims, preferred_element_type=f32)
    total += lax.dot_general(a[1], b[0], dims, preferred_element_type=f32)
    return total + lax.dot_general(a[0], b[0], dims, preferred_element_type=f32)


def step_kernel(
    coords, factor, out, place_ref, fv, fhigh, flow, pan, high, low, u, dgat, dall, dsmall, dy, dpart, ybuf, gout, gbuf, points, upd,
    work, tile, inv, linv, xs, xt, local, sz, rz, sdy, rdy, sdg, rdg, sy, ry, sg, rg, sx, rx, *sems,
):
    h, r, c, z, x, core = place()
    f32 = jnp.float32
    load = pltpu.make_async_copy(factor, fv, local.at[0])
    rows = pltpu.make_async_copy(factor.at[0, 0, pl.ds(0, PAN), :], pan.at[z, x, core, :, pl.ds(0, DEPTH)], local.at[1])
    where = pltpu.make_async_copy(coords, place_ref, local.at[3])
    where.start()
    rows.start()
    load.start()
    greeted = greet()
    where.wait()

    sub = lax.broadcasted_iota(jnp.int32, (PAN, 128), 0)
    lane = lax.broadcasted_iota(jnp.int32, (PAN, 128), 1)
    start = place_ref[:, :128].astype(f32) / GRID
    mark = jnp.zeros((PAN, 128), f32)
    own_x, own_y = mark, mark
    for j in range(PAN):
        px = jnp.broadcast_to(start[0:1, j : j + 1], (PAN, 128))
        py = jnp.broadcast_to(start[1:2, j : j + 1], (PAN, 128))
        own_x = jnp.where(sub == j, px, own_x)
        own_y = jnp.where(sub == j, py, own_y)
        both = jnp.where(sub == 0, px, jnp.where(sub == 1, py, 0.0))
        mark = jnp.where(lane == (r % 16) * PAN + j, both, mark)
    pan[z, x, core, :, DEPTH:] = mark
    rows.wait()
    greeted()

    first = Gather(pan, *sems[:4])
    second = Gather(dgat, *sems[4:])

    def panel_copy(source, target):
        block = pan.at[source, x, core]
        return send(block, block, sz.at[target], rz.at[source], {"row": target * 8 + x * 2 + core})

    def panel_each(act):
        def ring(k, carry):
            @pl.when(z >= k)
            def _():
                act(panel_copy(z, z - k))

            @pl.when(z + k < NZ)
            def _():
                act(panel_copy(z, z + k))

            return carry

        lax.fori_loop(1, NZ, ring, 0)

    panel_each(lambda copy: copy.start())
    load.wait()

    def panel_fetch(source):
        @pl.when(source != z)
        def _():
            panel_copy(source, z).wait_recv()

    def split(k):
        @pl.when(k < 8)
        def _():
            fhigh[k // 2, k % 2], flow[k // 2, k % 2] = halves(fv[k // 2, k % 2])

    def arrived(source):
        at = pl.ds(pl.multiple_of(source * 64, 64), 64)
        high[at, :], low[at, :] = halves(pan[source, :, :, :, :DEPTH].reshape(64, DEPTH))

    first.run(lambda k: k, panel_fetch, split, arrived)

    def y_small(e):
        return send(dsmall, dy.at[e - 1], sdy.at[e - 1], rdy.at[e - 1], {"col": (c + e) % NCOL})

    def y_large(s, e):
        part = (c + e) % NCOL
        return send(u.at[part, s], ybuf.at[s, e - 1], sy.at[s, e - 1], ry.at[s, e - 1], {"col": part})

    ring_place = h * NZ + z

    def part_copy(source, target):
        block = dpart.at[source]
        return send(block, block, sdg.at[target], rdg.at[source],
                    {"gen": target // NZ, "row": target % NZ * 8 + x * 2 + core})

    def part_each(act):
        def ring(k, carry):
            act(part_copy(ring_place, (ring_place + k) % (2 * NZ)))

            @pl.when(k < NZ)
            def _():
                act(part_copy(ring_place, (ring_place + 2 * NZ - k) % (2 * NZ)))

            return carry

        lax.fori_loop(1, NZ + 1, ring, 0)

    def part_fetch(source):
        for g in range(2):
            @pl.when(ring_place != g * NZ + source)
            def _():
                part_copy(g * NZ + source, ring_place).wait_recv()

        dgat[source, x, core] = dpart[source] + dpart[NZ + source]

    gen_large = send(gout, gbuf, sg.at[0], rg.at[0], {"gen": 1 - h})

    def tile_of(i):
        return (z // 2 + i) % 4

    def multiply(s):
        a = [part[:, s].reshape(4 * HALF, DEPTH) for part in (fhigh, flow)]
        u[:, s] = three(a, (high[...], low[...])).reshape(4, HALF, B)

    top = [part[0, 0, :16] for part in (fhigh, flow)]
    rows8 = three(top, (high[...], low[...]))[:PAN]
    for q in range(4):
        dall[q] = rows8[:, 128 * q : 128 * q + 128]
    for i in range(3):
        dsmall[i] = dall[tile_of(i)]
    for e in range(1, NCOL):
        y_small(e).start()
    grouped = pan[:, :, :, :, DEPTH:].reshape(4, 16, PAN, 128)
    for q in range(4):
        total = grouped[q, 0]
        for i in range(1, 16):
            total = total + grouped[q, i]
        points[q] = total
    kern = []
    for i in range(3):
        marked = points[tile_of(i)]
        same = jnp.where(lane + 128 * tile_of(i) == sub + PAN * r, f32(nugget_term), f32(0))
        kern.append(matern(own_x - marked[0:1], own_y - marked[1:2]) + same)
    multiply(0)
    for e in range(1, NCOL):
        y_small(e).wait_recv()
    for i in range(3):
        total = dsmall[i] + dy[0, i] + dy[1, i] + dy[2, i]
        dpart[ring_place, i] = jnp.where(h == 0, kern[i], 0.0) - total
    part_each(lambda copy: copy.start())

    @pl.when(h == 1)
    def _():
        for e in range(1, NCOL):
            y_large(0, e).start()

    multiply(1)

    @pl.when(h == 0)
    def _():
        for e in range(1, NCOL):
            y_large(1, e).start()

    here = pl.ds(pl.multiple_of((c * 2 + h) * HALF, HALF), HALF)
    mx = jnp.broadcast_to(place_ref[0:1, here].astype(f32) / GRID, (HALF, HALF)).T
    my = jnp.broadcast_to(place_ref[1:2, here].astype(f32) / GRID, (HALF, HALF)).T
    isub = lax.broadcasted_iota(jnp.int32, (HALF, 128), 0) + (c * 2 + h) * HALF
    ilane = lax.broadcasted_iota(jnp.int32, (HALF, 128), 1)
    for q in range(4):
        at = slice(128 * q, 128 * q + 128)
        same = (isub < PAN) & (ilane + 128 * q == isub + PAN * r)
        k = matern(mx - points[q, 0:1], my - points[q, 1:2]) + jnp.where(same, f32(nugget_term), f32(0))
        upd[:, at] = k
    linv[...] = jnp.zeros((B, B), f32)
    def pass_on(k):
        @pl.when(k == NZ - 1)
        def _():
            for e in range(1, NCOL):
                y_large(1 - h, e).wait_recv()
            gout[...] = u[c, 1 - h] + ybuf[1 - h, 0] + ybuf[1 - h, 1] + ybuf[1 - h, 2]
            gen_large.start()
            for e in range(1, NCOL):
                y_large(h, e).start()

    second.run(lambda k: NZ // 2 + ((k + 1) // 2) * (1 - 2 * (k % 2)), part_fetch, pass_on)
    for t, i in ((0, 0), (0, 1), (0, 2), (1, 0), (1, 1), (1, 2), (2, 0), (2, 1), (3, 0), (3, 1)):
        block = dgat[2 * t : 2 * t + 2, :, :, i].reshape(128, 128)
        if t + i == 4:
            block, row, col = block.T, 0, 3
        else:
            row, col = t, t + i
        work[128 * row : 128 * row + 128, 128 * col : 128 * col + 128] = block

    def combine():
        for e in range(1, NCOL):
            y_large(h, e).wait_recv()
        for q in range(4):
            at = slice(128 * q, 128 * q + 128)
            part = u[c, h, :, at] + ybuf[h, 0, :, at] + ybuf[h, 1, :, at] + ybuf[h, 2, :, at]
            upd[:, at] = upd[:, at] - part

    def settle():
        gen_large.wait_recv()
        upd[...] = upd[...] - gbuf[...]

    slot = c * 2 + h

    def deliver(g):
        return send(
            xs.at[g], xt.at[slot], sx.at[g], rx.at[slot], {"gen": g // NCOL, "col": g % NCOL}
        )

    def solve(v):
        lo, hi = 128 * v, 128 * v + 128
        block = dotf(linv[lo:hi, :hi], upd[:, :hi], ((1,), (1,)))
        for i in range(2):
            g = 2 * v + i
            xs[g] = block[64 * i : 64 * i + 64]

            @pl.when(h * NCOL + c == g)
            def _():
                xt[slot] = xs[g]

            @pl.when(h * NCOL + c != g)
            def _():
                deliver(g).start()

    def step(k, carry):
        for v in range(4):
            @pl.when(k == v)
            def _():
                tile[...] = work[128 * v : 128 * v + 128, 128 * v : 128 * v + 128]
        inverse_factor(tile, inv)
        for v in range(4):
            @pl.when(k == v)
            def _():
                lo, hi = 128 * v, 128 * v + 128
                t = inv[...]
                if v:
                    linv[lo:hi, :lo] = dotf(t, linv[lo:hi, :lo], ((1,), (0,)))
                linv[lo:hi, lo:hi] = t
                if v < 3:
                    p = dotf(t, work[lo:hi, hi:], ((1,), (0,)))
                    for w in range(v + 1, 4):
                        at = slice(128 * w, 128 * w + 128)
                        left = slice(128 * w - hi, 128 * w + 128 - hi)
                        work[at, 128 * w :] = work[at, 128 * w :] - dotf(p[:, left], p[:, 128 * w - hi :], ((0,), (0,)))
                    linv[hi:, :hi] = linv[hi:, :hi] - dotf(p, linv[lo:hi, :hi], ((0,), (0,)))
                if v == 1:
                    combine()
                    settle()
                    solve(0)
                if v:
                    solve(v)
        return carry

    lax.fori_loop(0, 4, step, 0)
    for e in range(1, NCOL):
        y_small(e).wait_send()
        for s in range(2):
            y_large(s, e).wait_send()
    part_each(lambda copy: copy.wait_send())
    panel_each(lambda copy: copy.wait_send())
    gen_large.wait_send()
    first.finish()
    second.finish()

    for g in range(2 * NCOL):
        @pl.when(h * NCOL + c != g)
        def _():
            theirs = (g % NCOL) * 2 + g // NCOL
            send(xs.at[g], xt.at[theirs], sx.at[g], rx.at[theirs], {"gen": g // NCOL, "col": g % NCOL}).wait_recv()

    for i in range(2 * NCOL):
        out[:, HALF * i : HALF * i + HALF] = xt[i]

    for g in range(2 * NCOL):
        @pl.when(h * NCOL + c != g)
        def _():
            deliver(g).wait_send()


def shards(coords, factor):
    dma = pltpu.SemaphoreType.DMA
    vmem = pl.BlockSpec(memory_space=pltpu.VMEM)

    def room(*shape, dtype=jnp.float32):
        return pltpu.VMEM(shape, dtype)

    solved = pl.pallas_call(
        step_kernel,
        out_shape=jax.ShapeDtypeStruct((B // 8, ROWS), jnp.float32),
        in_specs=[pl.BlockSpec(memory_space=pltpu.HBM)] * 2,
        out_specs=vmem,
        scratch_shapes=[
            room(2, ROWS, dtype=jnp.int32),
            room(4, 2, HALF, DEPTH),
            room(4, 2, HALF, DEPTH, dtype=jnp.bfloat16),
            room(4, 2, HALF, DEPTH, dtype=jnp.bfloat16),
            room(NZ, NX, NC, PAN, WIDE),
            room(B, DEPTH, dtype=jnp.bfloat16),
            room(B, DEPTH, dtype=jnp.bfloat16),
            room(4, 2, HALF, B),
            room(NZ, NX, NC, 3, PAN, 128),
            room(4, PAN, 128),
            room(3, PAN, 128),
            room(NCOL - 1, 3, PAN, 128),
            room(2 * NZ, 3, PAN, 128),
            room(2, NCOL - 1, HALF, B),
            room(HALF, B),
            room(HALF, B),
            room(4, PAN, 128),
            room(HALF, B),
            room(B, B),
            room(128, 128),
            room(128, 128),
            room(B, B),
            room(2 * NCOL, B // 8, HALF),
            room(2 * NCOL, B // 8, HALF),
            dma((4,)), dma((NZ,)), dma((NZ,)), dma((3,)), dma((3,)), dma((2 * NZ,)), dma((2 * NZ,)), dma((2, 3)), dma((2, 3)),
            dma((1,)), dma((1,)), dma((8,)), dma((8,)),
            *gather_sems(), *gather_sems(),
        ],
        compiler_params=pltpu.CompilerParams(
            collective_id=0, has_side_effects=True, vmem_limit_bytes=60 << 20
        ),
        name="panel_step",
    )(coords, factor.reshape(4, 2, HALF, DEPTH))
    return solved.T


def solution(mesh):
    in_specs = (P(None, "row"), P("row", ("gen", "col")))
    out_specs = P("row", ("gen", "col"))
    return jax.shard_map(shards, mesh=mesh, in_specs=in_specs, out_specs=out_specs, check_vma=False)
```

```python
import jax
import jax.numpy as jnp
from jax import lax
from jax.experimental import pallas as pl
from jax.experimental.pallas import tpu as pltpu
from jax.sharding import PartitionSpec as P

B = 512
GRID = 1024
PAN = 8
ROWS = 1024
DEPTH = 1024
HALF = 128
LAG = 2
NZ, NX, NC, NCOL = 8, 4, 2, 4
WIDE = DEPTH + 128

root_three = 1.7320508075688772
length_scale = 0.2
nugget_term = 1.0

HI = lax.Precision.HIGHEST
MESH = pl.DeviceIdType.MESH


def dotf(a, b, dims):
    return lax.dot_general(a, b, (dims, ((), ())), precision=HI, preferred_element_type=jnp.float32)


def matern(delta_x, delta_y):
    scaled = root_three * jnp.sqrt(delta_x * delta_x + delta_y * delta_y) / length_scale
    return (1.0 + scaled) * jnp.exp(-scaled)


def spread(x, k):
    return jnp.broadcast_to(x[k : k + 1], x.shape)


def inverse_factor(tile_ref, out_ref):
    sub = lax.broadcasted_iota(jnp.int32, (8, 128), 0)
    lane = lax.broadcasted_iota(jnp.int32, (8, 128), 1)
    a = [tile_ref[8 * i : 8 * i + 8, :] for i in range(16)]
    t = [jnp.where(lane == sub + 8 * i, jnp.float32(1), jnp.float32(0)) for i in range(16)]
    for b in range(16):
        cols = [jnp.broadcast_to(a[b][:, 8 * b + k : 8 * b + k + 1], (8, 128)) for k in range(8)]
        recip, cross, scale = [], [], jnp.ones((8, 128), jnp.float32)
        for k in range(8):
            pivot = spread(cols[k], k)
            r = 1.0 / pivot
            recip.append(r)
            scale = jnp.where(sub == k, pivot, scale)
            m = jnp.where(sub > k, cols[k] * r, 0.0)
            row = []
            for j in range(k + 1, 8):
                s = spread(cols[j], k)
                row.append(s)
                cols[j] = cols[j] - m * s
            cross.append(row)
            a[b] = a[b] - m * spread(a[b], k)
            t[b] = t[b] - m * spread(t[b], k)
        ua = [spread(a[b], k) for k in range(8)]
        ut = [spread(t[b], k) for k in range(8)]
        out_ref[8 * b : 8 * b + 8, :] = t[b] * lax.rsqrt(scale)
        inverse_pivots = jnp.ones((8, 128), jnp.float32)
        for k in range(8):
            inverse_pivots = jnp.where(sub == k, recip[k], inverse_pivots)
        scaled = a[b] * inverse_pivots
        for i in range(b + 1, min(b + 1 + 2, 16)):
            c = [jnp.broadcast_to(a[i][:, 8 * b + k : 8 * b + k + 1], (8, 128)) for k in range(8)]
            da = dt = None
            for k in range(8):
                m = c[k] * recip[k]
                for j in range(k + 1, 8):
                    c[j] = c[j] - m * cross[k][j - k - 1]
                da = m * ua[k] if da is None else da + m * ua[k]
                dt = m * ut[k] if dt is None else dt + m * ut[k]
            a[i] = a[i] - da
            t[i] = t[i] - dt
        if b + 1 + 2 < 16:
            hi = scaled.astype(jnp.bfloat16).astype(jnp.float32); r1 = scaled - hi
            mi = r1.astype(jnp.bfloat16).astype(jnp.float32); lo = r1 - mi
            both = jnp.concatenate([a[b], t[b]], axis=1)
            bh = both.astype(jnp.bfloat16).astype(jnp.float32); r2 = both - bh
            bm = r2.astype(jnp.bfloat16).astype(jnp.float32); bl = r2 - bm
            lhs = jnp.concatenate([hi, hi, mi, hi, lo, mi, hi, hi], axis=0).astype(jnp.bfloat16)
            rhs = jnp.concatenate([bh, bm, bh, bl, bh, bm, 0 * bh, 0 * bh], axis=0).astype(jnp.bfloat16)
            delta = lax.dot_general(lhs, rhs, (((0,), (0,)), ((), ())), preferred_element_type=jnp.float32)
            for i in range(b + 1 + 2, 16):
                a[i] = a[i] - delta[8 * i : 8 * i + 8, :128]
                t[i] = t[i] - delta[8 * i : 8 * i + 8, 128:]
def place():
    h, r, c = lax.axis_index("gen"), lax.axis_index("row"), lax.axis_index("col")
    return h, r, c, r // 8, (r // 2) % 4, r % 2


def send(src, dst, send_sem, recv_sem, where):
    return pltpu.make_async_remote_copy(
        src_ref=src, dst_ref=dst, send_sem=send_sem, recv_sem=recv_sem, device_id=where, device_id_type=MESH
    )


class Gather:
    def __init__(self, buf, sx, rx, sc, rc):
        self.buf, self.sx, self.rx, self.sc, self.rc = buf, sx, rx, sc, rc
        _, self.r, _, self.z, self.x, self.core = place()

    def along_x(self, source, e):
        target = (self.x + e) % NX
        block = self.buf.at[source, self.x, self.core]
        return send(block, block, self.sx.at[source, e - 1], self.rx.at[source, self.x],
                    {"row": self.z * 8 + target * 2 + self.core})

    def from_x(self, source, e):
        x = (self.x + e) % NX
        block = self.buf.at[source, x, self.core]
        return send(block, block, self.sx.at[source, 0], self.rx.at[source, x], {"row": self.r + 1 - 2 * self.core})

    def across(self, source, core):
        block = self.buf.at[source, :, core]
        return send(block, block, self.sc.at[source], self.rc.at[source], {"row": self.r + 1 - 2 * self.core})

    def run(self, away, fetch, aside, arrived=None):
        z = self.z

        def forward(source):
            fetch(source)
            for e in range(1, NX):
                self.along_x(source, e).start()

        def swap(source):
            for e in range(1, NX):
                self.from_x(source, e).wait_recv()
            self.across(source, self.core).start()

        def arrive(source):
            self.across(source, 1 - self.core).wait_recv()
            if arrived is not None:
                arrived(source)

        def visit(act, k):
            d = away(k)
            inside = (k >= 0) & (k < NZ)

            @pl.when(inside & (z >= d))
            def _():
                act(z - d)

            @pl.when(inside & (d > 0) & (z + d < NZ))
            def _():
                act(z + d)

        def ring(k, carry):
            visit(forward, k)
            aside(k)
            visit(swap, k - LAG)
            return carry

        def last(k, carry):
            visit(arrive, k)
            return carry

        lax.fori_loop(0, NZ + LAG, ring, 0)
        lax.fori_loop(0, NZ, last, 0)

    def finish(self):
        def drain(source, carry):
            for e in range(1, NX):
                self.along_x(source, e).wait_send()
            self.across(source, self.core).wait_send()
            return carry

        lax.fori_loop(0, NZ, drain, 0)


def gather_sems():
    dma = pltpu.SemaphoreType.DMA
    return [dma((NZ, NX - 1)), dma((NZ, NX)), dma((NZ,)), dma((NZ,))]


def greet():
    h, r, c, z, x, core = place()
    barrier = pltpu.get_barrier_semaphore()
    peers = [{"row": (z + d) % NZ * 8 + x * 2 + core} for d in range(1, NZ)]
    peers += [{"row": z * 8 + (x + e) % NX * 2 + core} for e in range(1, NX)]
    peers += [{"row": r + 1 - 2 * core}]
    peers += [{"col": (c + e) % NCOL} for e in range(1, NCOL)]
    peers += [{"gen": 1 - h, "col": (c + e) % NCOL} for e in range(NCOL)]
    peers += [{"gen": 1 - h, "row": (z + d) % NZ * 8 + x * 2 + core} for d in range(1, NZ)]
    for peer in peers:
        pl.semaphore_signal(barrier, inc=1, device_id=peer, device_id_type=MESH)
    return lambda: pl.semaphore_wait(barrier, len(peers))


def halves(x):
    high = x.astype(jnp.bfloat16)
    return high, (x - high.astype(jnp.float32)).astype(jnp.bfloat16)


def three(a, b):
    dims = (((1,), (1,)), ((), ()))
    f32 = jnp.float32
    total = lax.dot_general(a[0], b[1], dims, preferred_element_type=f32)
    total += lax.dot_general(a[1], b[0], dims, preferred_element_type=f32)
    return total + lax.dot_general(a[0], b[0], dims, preferred_element_type=f32)


def step_kernel(
    coords, factor, out, place_ref, fv, fhigh, flow, pan, high, low, u, dgat, dall, dsmall, dy, dpart, ybuf, gout, gbuf, points, upd,
    work, inv, linv, xs, xt, local, sz, rz, sdy, rdy, sdg, rdg, sy, ry, sg, rg, sx, rx, *sems,
):
    h, r, c, z, x, core = place()
    f32 = jnp.float32
    load = pltpu.make_async_copy(factor, fv, local.at[0])
    rows = pltpu.make_async_copy(factor.at[0, 0, pl.ds(0, PAN), :], pan.at[z, x, core, :, pl.ds(0, DEPTH)], local.at[1])
    greeted = greet()
    where = pltpu.make_async_copy(coords, place_ref, local.at[3])
    where.start()
    rows.start()
    load.start()
    where.wait()

    sub = lax.broadcasted_iota(jnp.int32, (PAN, 128), 0)
    lane = lax.broadcasted_iota(jnp.int32, (PAN, 128), 1)
    start = place_ref[:, :128].astype(f32) / GRID
    mark = jnp.zeros((PAN, 128), f32)
    own_x, own_y = mark, mark
    for j in range(PAN):
        px = jnp.broadcast_to(start[0:1, j : j + 1], (PAN, 128))
        py = jnp.broadcast_to(start[1:2, j : j + 1], (PAN, 128))
        own_x = jnp.where(sub == j, px, own_x)
        own_y = jnp.where(sub == j, py, own_y)
        both = jnp.where(sub == 0, px, jnp.where(sub == 1, py, 0.0))
        mark = jnp.where(lane == (r % 16) * PAN + j, both, mark)
    pan[z, x, core, :, DEPTH:] = mark
    rows.wait()
    greeted()

    first = Gather(pan, *sems[:4])
    second = Gather(dgat, *sems[4:])

    def panel_copy(source, target):
        block = pan.at[source, x, core]
        return send(block, block, sz.at[target], rz.at[source], {"row": target * 8 + x * 2 + core})

    def panel_each(act):
        def ring(k, carry):
            @pl.when(z >= k)
            def _():
                act(panel_copy(z, z - k))

            @pl.when(z + k < NZ)
            def _():
                act(panel_copy(z, z + k))

            return carry

        lax.fori_loop(1, NZ, ring, 0)

    panel_each(lambda copy: copy.start())
    load.wait()

    def panel_fetch(source):
        @pl.when(source != z)
        def _():
            panel_copy(source, z).wait_recv()

    def split(k):
        @pl.when(k < 8)
        def _():
            fhigh[k // 2, k % 2], flow[k // 2, k % 2] = halves(fv[k // 2, k % 2])

    def arrived(source):
        at = pl.ds(pl.multiple_of(source * 64, 64), 64)
        high[at, :], low[at, :] = halves(pan[source, :, :, :, :DEPTH].reshape(64, DEPTH))

    first.run(lambda k: k, panel_fetch, split, arrived)

    def y_small(e):
        return send(dsmall, dy.at[e - 1], sdy.at[e - 1], rdy.at[e - 1], {"col": (c + e) % NCOL})

    def y_large(s, e):
        part = (c + e) % NCOL
        return send(u.at[part, s], ybuf.at[s, e - 1], sy.at[s, e - 1], ry.at[s, e - 1], {"col": part})

    ring_place = h * NZ + z

    def part_copy(source, target):
        block = dpart.at[source]
        return send(block, block, sdg.at[target], rdg.at[source],
                    {"gen": target // NZ, "row": target % NZ * 8 + x * 2 + core})

    def part_each(act):
        def ring(k, carry):
            act(part_copy(ring_place, (ring_place + k) % (2 * NZ)))

            @pl.when(k < NZ)
            def _():
                act(part_copy(ring_place, (ring_place + 2 * NZ - k) % (2 * NZ)))

            return carry

        lax.fori_loop(1, NZ + 1, ring, 0)

    def part_fetch(source):
        for g in range(2):
            @pl.when(ring_place != g * NZ + source)
            def _():
                part_copy(g * NZ + source, ring_place).wait_recv()

        dgat[source, x, core] = dpart[source] + dpart[NZ + source]

    gen_large = send(gout, gbuf, sg.at[0], rg.at[0], {"gen": 1 - h})

    def tile_of(i):
        return (z // 2 + i) % 4

    def multiply(s):
        a = [part[:, s].reshape(4 * HALF, DEPTH) for part in (fhigh, flow)]
        u[:, s] = three(a, (high[...], low[...])).reshape(4, HALF, B)

    top = [part[0, 0, :16] for part in (fhigh, flow)]
    rows8 = three(top, (high[...], low[...]))[:PAN]
    for q in range(4):
        dall[q] = rows8[:, 128 * q : 128 * q + 128]
    for i in range(3):
        dsmall[i] = dall[tile_of(i)]
    for e in range(1, NCOL):
        y_small(e).start()
    grouped = pan[:, :, :, :, DEPTH:].reshape(4, 16, PAN, 128)
    for q in range(4):
        total = grouped[q, 0]
        for i in range(1, 16):
            total = total + grouped[q, i]
        points[q] = total
    kern = []
    for i in range(3):
        marked = points[tile_of(i)]
        same = jnp.where(lane + 128 * tile_of(i) == sub + PAN * r, f32(nugget_term), f32(0))
        kern.append(matern(own_x - marked[0:1], own_y - marked[1:2]) + same)
    multiply(0)
    for e in range(1, NCOL):
        y_small(e).wait_recv()
    for i in range(3):
        total = dsmall[i] + dy[0, i] + dy[1, i] + dy[2, i]
        dpart[ring_place, i] = jnp.where(h == 0, kern[i], 0.0) - total
    part_each(lambda copy: copy.start())

    @pl.when(h == 1)
    def _():
        for e in range(1, NCOL):
            y_large(0, e).start()

    multiply(1)

    @pl.when(h == 0)
    def _():
        for e in range(1, NCOL):
            y_large(1, e).start()

    here = pl.ds(pl.multiple_of((c * 2 + h) * HALF, HALF), HALF)
    mx = jnp.broadcast_to(place_ref[0:1, here].astype(f32) / GRID, (HALF, HALF)).T
    my = jnp.broadcast_to(place_ref[1:2, here].astype(f32) / GRID, (HALF, HALF)).T
    isub = lax.broadcasted_iota(jnp.int32, (HALF, 128), 0) + (c * 2 + h) * HALF
    ilane = lax.broadcasted_iota(jnp.int32, (HALF, 128), 1)
    for q in range(4):
        at = slice(128 * q, 128 * q + 128)
        same = (isub < PAN) & (ilane + 128 * q == isub + PAN * r)
        k = matern(mx - points[q, 0:1], my - points[q, 1:2]) + jnp.where(same, f32(nugget_term), f32(0))
        upd[:, at] = k
    linv[...] = jnp.zeros((B, B), f32)
    def pass_on(k):
        @pl.when(k == NZ - 1)
        def _():
            for e in range(1, NCOL):
                y_large(1 - h, e).wait_recv()
            gout[...] = u[c, 1 - h] + ybuf[1 - h, 0] + ybuf[1 - h, 1] + ybuf[1 - h, 2]
            gen_large.start()
            for e in range(1, NCOL):
                y_large(h, e).start()

    second.run(lambda k: NZ // 2 + ((k + 1) // 2) * (1 - 2 * (k % 2)), part_fetch, pass_on)
    for t, i in ((0, 0), (0, 1), (0, 2), (1, 0), (1, 1), (1, 2), (2, 0), (2, 1), (3, 0), (3, 1)):
        block = dgat[2 * t : 2 * t + 2, :, :, i].reshape(128, 128)
        if t + i == 4:
            block, row, col = block.T, 0, 3
        else:
            row, col = t, t + i
        work[128 * row : 128 * row + 128, 128 * col : 128 * col + 128] = block

    def combine():
        for e in range(1, NCOL):
            y_large(h, e).wait_recv()
        for q in range(4):
            at = slice(128 * q, 128 * q + 128)
            part = u[c, h, :, at] + ybuf[h, 0, :, at] + ybuf[h, 1, :, at] + ybuf[h, 2, :, at]
            upd[:, at] = upd[:, at] - part

    def settle():
        gen_large.wait_recv()
        upd[...] = upd[...] - gbuf[...]

    slot = c * 2 + h

    def deliver(g):
        return send(
            xs.at[g], xt.at[slot], sx.at[g], rx.at[slot], {"gen": g // NCOL, "col": g % NCOL}
        )

    def solve(v):
        lo, hi = 128 * v, 128 * v + 128
        block = dotf(linv[lo:hi, :hi], upd[:, :hi], ((1,), (1,)))
        for i in range(2):
            g = 2 * v + i
            xs[g] = block[64 * i : 64 * i + 64]

            @pl.when(h * NCOL + c == g)
            def _():
                xt[slot] = xs[g]

            @pl.when(h * NCOL + c != g)
            def _():
                deliver(g).start()

    later = None
    for v in range(4):
        lo, hi = 128 * v, 128 * v + 128
        inverse_factor(work.at[lo:hi, lo:hi], inv.at[v])
        if later is not None:
            later()
        t = inv[v]
        if v < 3:
            p = dotf(t, work[lo:hi, hi:], ((1,), (0,)))
            near = slice(hi, hi + 128)
            work[near, near] = work[near, near] - dotf(p[:, :128], p[:, :128], ((0,), (0,)))
        if v:
            linv[lo:hi, :lo] = dotf(t, linv[lo:hi, :lo], ((1,), (0,)))
        linv[lo:hi, lo:hi] = t

        def later(p=p, lo=lo, hi=hi):
            for w in range(hi // 128, 4):
                at = slice(128 * w, 128 * w + 128)
                left = slice(128 * w - hi, 128 * w + 128 - hi)
                first_col = max(128 * w, hi + 128)
                if first_col < B and (w > hi // 128 or first_col > 128 * w):
                    work[at, first_col:] = work[at, first_col:] - dotf(p[:, left], p[:, first_col - hi :], ((0,), (0,)))
            if hi < B:
                linv[hi:, :hi] = linv[hi:, :hi] - dotf(p, linv[lo:hi, :hi], ((0,), (0,)))

        if v == 1:
            combine()
            settle()
            solve(0)
        if v:
            solve(v)

    for e in range(1, NCOL):
        y_small(e).wait_send()
        for s in range(2):
            y_large(s, e).wait_send()
    part_each(lambda copy: copy.wait_send())
    panel_each(lambda copy: copy.wait_send())
    gen_large.wait_send()
    first.finish()
    second.finish()

    for g in range(2 * NCOL):
        @pl.when(h * NCOL + c != g)
        def _():
            theirs = (g % NCOL) * 2 + g // NCOL
            send(xs.at[g], xt.at[theirs], sx.at[g], rx.at[theirs], {"gen": g // NCOL, "col": g % NCOL}).wait_recv()

    for i in range(2 * NCOL):
        out[:, HALF * i : HALF * i + HALF] = xt[i]

    for g in range(2 * NCOL):
        @pl.when(h * NCOL + c != g)
        def _():
            deliver(g).wait_send()


def shards(coords, factor):
    dma = pltpu.SemaphoreType.DMA
    vmem = pl.BlockSpec(memory_space=pltpu.VMEM)

    def room(*shape, dtype=jnp.float32):
        return pltpu.VMEM(shape, dtype)

    solved = pl.pallas_call(
        step_kernel,
        out_shape=jax.ShapeDtypeStruct((B // 8, ROWS), jnp.float32),
        in_specs=[pl.BlockSpec(memory_space=pltpu.HBM)] * 2,
        out_specs=vmem,
        scratch_shapes=[
            room(2, ROWS, dtype=jnp.int32),
            room(4, 2, HALF, DEPTH),
            room(4, 2, HALF, DEPTH, dtype=jnp.bfloat16),
            room(4, 2, HALF, DEPTH, dtype=jnp.bfloat16),
            room(NZ, NX, NC, PAN, WIDE),
            room(B, DEPTH, dtype=jnp.bfloat16),
            room(B, DEPTH, dtype=jnp.bfloat16),
            room(4, 2, HALF, B),
            room(NZ, NX, NC, 3, PAN, 128),
            room(4, PAN, 128),
            room(3, PAN, 128),
            room(NCOL - 1, 3, PAN, 128),
            room(2 * NZ, 3, PAN, 128),
            room(2, NCOL - 1, HALF, B),
            room(HALF, B),
            room(HALF, B),
            room(4, PAN, 128),
            room(HALF, B),
            room(B, B),
            room(4, 128, 128),
            room(B, B),
            room(2 * NCOL, B // 8, HALF),
            room(2 * NCOL, B // 8, HALF),
            dma((4,)), dma((NZ,)), dma((NZ,)), dma((3,)), dma((3,)), dma((2 * NZ,)), dma((2 * NZ,)), dma((2, 3)), dma((2, 3)),
            dma((1,)), dma((1,)), dma((8,)), dma((8,)),
            *gather_sems(), *gather_sems(),
        ],
        compiler_params=pltpu.CompilerParams(
            collective_id=0, has_side_effects=True, vmem_limit_bytes=60 << 20
        ),
        name="panel_step",
    )(coords, factor.reshape(4, 2, HALF, DEPTH))
    return solved.T


def solution(mesh):
    in_specs = (P(None, "row"), P("row", ("gen", "col")))
    out_specs = P("row", ("gen", "col"))
    return jax.shard_map(shards, mesh=mesh, in_specs=in_specs, out_specs=out_specs, check_vma=False)
```

```python
import jax
import jax.numpy as jnp
from jax import lax
from jax.experimental import pallas as pl
from jax.experimental.pallas import tpu as pltpu
from jax.sharding import PartitionSpec as P

B = 512
GRID = 1024
PAN = 8
ROWS = 1024
DEPTH = 1024
HALF = 128
NZ, NX, NC, NCOL = 8, 4, 2, 4
WIDE = DEPTH + 128

root_three = 1.7320508075688772
length_scale = 0.2
nugget_term = 1.0

HI = lax.Precision.HIGHEST
MESH = pl.DeviceIdType.MESH


def dotf(a, b, dims):
    return lax.dot_general(a, b, (dims, ((), ())), precision=HI, preferred_element_type=jnp.float32)


def matern(delta_x, delta_y):
    scaled = root_three * jnp.sqrt(delta_x * delta_x + delta_y * delta_y) / length_scale
    return (1.0 + scaled) * jnp.exp(-scaled)


def spread(x, k):
    return jnp.broadcast_to(x[k : k + 1], x.shape)


def inverse_factor(tile_ref, out_ref):
    sub = lax.broadcasted_iota(jnp.int32, (8, 128), 0)
    lane = lax.broadcasted_iota(jnp.int32, (8, 128), 1)
    a = [tile_ref[8 * i : 8 * i + 8, :] for i in range(16)]
    t = [jnp.where(lane == sub + 8 * i, jnp.float32(1), jnp.float32(0)) for i in range(16)]
    for b in range(16):
        cols = [jnp.broadcast_to(a[b][:, 8 * b + k : 8 * b + k + 1], (8, 128)) for k in range(8)]
        recip, cross, scale = [], [], jnp.ones((8, 128), jnp.float32)
        for k in range(8):
            pivot = spread(cols[k], k)
            r = 1.0 / pivot
            recip.append(r)
            scale = jnp.where(sub == k, pivot, scale)
            m = jnp.where(sub > k, cols[k] * r, 0.0)
            row = []
            for j in range(k + 1, 8):
                s = spread(cols[j], k)
                row.append(s)
                cols[j] = cols[j] - m * s
            cross.append(row)
            a[b] = a[b] - m * spread(a[b], k)
            t[b] = t[b] - m * spread(t[b], k)
        ua = [spread(a[b], k) for k in range(8)]
        ut = [spread(t[b], k) for k in range(8)]
        out_ref[8 * b : 8 * b + 8, :] = t[b] * lax.rsqrt(scale)
        inverse_pivots = jnp.ones((8, 128), jnp.float32)
        for k in range(8):
            inverse_pivots = jnp.where(sub == k, recip[k], inverse_pivots)
        scaled = a[b] * inverse_pivots
        for i in range(b + 1, min(b + 1 + 2, 16)):
            c = [jnp.broadcast_to(a[i][:, 8 * b + k : 8 * b + k + 1], (8, 128)) for k in range(8)]
            da = dt = None
            for k in range(8):
                m = c[k] * recip[k]
                for j in range(k + 1, 8):
                    c[j] = c[j] - m * cross[k][j - k - 1]
                da = m * ua[k] if da is None else da + m * ua[k]
                dt = m * ut[k] if dt is None else dt + m * ut[k]
            a[i] = a[i] - da
            t[i] = t[i] - dt
        if b + 1 + 2 < 16:
            hi = scaled.astype(jnp.bfloat16).astype(jnp.float32); r1 = scaled - hi
            mi = r1.astype(jnp.bfloat16).astype(jnp.float32); lo = r1 - mi
            both = jnp.concatenate([a[b], t[b]], axis=1)
            bh = both.astype(jnp.bfloat16).astype(jnp.float32); r2 = both - bh
            bm = r2.astype(jnp.bfloat16).astype(jnp.float32); bl = r2 - bm
            lhs = jnp.concatenate([hi, hi, mi, hi, lo, mi, hi, hi], axis=0).astype(jnp.bfloat16)
            rhs = jnp.concatenate([bh, bm, bh, bl, bh, bm, 0 * bh, 0 * bh], axis=0).astype(jnp.bfloat16)
            delta = lax.dot_general(lhs, rhs, (((0,), (0,)), ((), ())), preferred_element_type=jnp.float32)
            for i in range(b + 1 + 2, 16):
                a[i] = a[i] - delta[8 * i : 8 * i + 8, :128]
                t[i] = t[i] - delta[8 * i : 8 * i + 8, 128:]
def place():
    h, r, c = lax.axis_index("gen"), lax.axis_index("row"), lax.axis_index("col")
    return h, r, c, r // 8, (r // 2) % 4, r % 2


def send(src, dst, send_sem, recv_sem, where):
    return pltpu.make_async_remote_copy(
        src_ref=src, dst_ref=dst, send_sem=send_sem, recv_sem=recv_sem, device_id=where, device_id_type=MESH
    )


class Gather:
    def __init__(self, buf, sx, rx, sc, rc):
        self.buf, self.sx, self.rx, self.sc, self.rc = buf, sx, rx, sc, rc
        _, self.r, _, self.z, self.x, self.core = place()

    def along_x(self, source, e):
        target = (self.x + e) % NX
        block = self.buf.at[source, self.x, self.core]
        return send(block, block, self.sx.at[source, e - 1], self.rx.at[source, self.x],
                    {"row": self.z * 8 + target * 2 + self.core})

    def from_x(self, source, e):
        x = (self.x + e) % NX
        block = self.buf.at[source, x, self.core]
        return send(block, block, self.sx.at[source, 0], self.rx.at[source, x], {"row": self.r + 1 - 2 * self.core})

    def across(self, source, core):
        block = self.buf.at[source, :, core]
        return send(block, block, self.sc.at[source], self.rc.at[source], {"row": self.r + 1 - 2 * self.core})

    def run(self, away, fetch, aside, arrived=None, lag=2):
        z = self.z

        def forward(source):
            fetch(source)
            for e in range(1, NX):
                self.along_x(source, e).start()

        def swap(source):
            for e in range(1, NX):
                self.from_x(source, e).wait_recv()
            self.across(source, self.core).start()

        def arrive(source):
            self.across(source, 1 - self.core).wait_recv()
            if arrived is not None:
                arrived(source)

        def visit(act, k):
            d = away(k)
            inside = (k >= 0) & (k < NZ)

            @pl.when(inside & (z >= d))
            def _():
                act(z - d)

            @pl.when(inside & (d > 0) & (z + d < NZ))
            def _():
                act(z + d)

        def ring(k, carry):
            visit(forward, k)
            aside(k)
            visit(swap, k - lag)
            return carry

        def last(k, carry):
            visit(arrive, k)
            return carry

        lax.fori_loop(0, NZ + lag, ring, 0)
        lax.fori_loop(0, NZ, last, 0)

    def finish(self):
        def drain(source, carry):
            for e in range(1, NX):
                self.along_x(source, e).wait_send()
            self.across(source, self.core).wait_send()
            return carry

        lax.fori_loop(0, NZ, drain, 0)


def gather_sems():
    dma = pltpu.SemaphoreType.DMA
    return [dma((NZ, NX - 1)), dma((NZ, NX)), dma((NZ,)), dma((NZ,))]


def greet():
    h, r, c, z, x, core = place()
    barrier = pltpu.get_barrier_semaphore()
    peers = [{"row": (z + d) % NZ * 8 + x * 2 + core} for d in range(1, NZ)]
    peers += [{"row": z * 8 + (x + e) % NX * 2 + core} for e in range(1, NX)]
    peers += [{"row": r + 1 - 2 * core}]
    peers += [{"col": (c + e) % NCOL} for e in range(1, NCOL)]
    peers += [{"gen": 1 - h, "col": (c + e) % NCOL} for e in range(NCOL)]
    peers += [{"gen": 1 - h, "row": (z + d) % NZ * 8 + x * 2 + core} for d in range(1, NZ)]
    for peer in peers:
        pl.semaphore_signal(barrier, inc=1, device_id=peer, device_id_type=MESH)
    return lambda: pl.semaphore_wait(barrier, len(peers))


def halves(x):
    high = x.astype(jnp.bfloat16)
    return high, (x - high.astype(jnp.float32)).astype(jnp.bfloat16)


def three(a, b):
    dims = (((1,), (1,)), ((), ()))
    f32 = jnp.float32
    total = lax.dot_general(a[0], b[1], dims, preferred_element_type=f32)
    total += lax.dot_general(a[1], b[0], dims, preferred_element_type=f32)
    return total + lax.dot_general(a[0], b[0], dims, preferred_element_type=f32)


def step_kernel(
    coords, factor, out, place_ref, fv, fhigh, flow, pan, high, low, u, dgat, dall, dsmall, dy, dpart, ybuf, gout, gbuf, points, upd,
    work, tile, inv, linv, xs, xt, local, sz, rz, sdy, rdy, sdg, rdg, sy, ry, sg, rg, sx, rx, *sems,
):
    h, r, c, z, x, core = place()
    f32 = jnp.float32
    load = pltpu.make_async_copy(factor, fv, local.at[0])
    rows = pltpu.make_async_copy(factor.at[0, 0, pl.ds(0, PAN), :], pan.at[z, x, core, :, pl.ds(0, DEPTH)], local.at[1])
    greeted = greet()
    where = pltpu.make_async_copy(coords, place_ref, local.at[3])
    where.start()
    rows.start()
    load.start()
    where.wait()

    sub = lax.broadcasted_iota(jnp.int32, (PAN, 128), 0)
    lane = lax.broadcasted_iota(jnp.int32, (PAN, 128), 1)
    start = place_ref[:, :128].astype(f32) / GRID
    mark = jnp.zeros((PAN, 128), f32)
    own_x, own_y = mark, mark
    for j in range(PAN):
        px = jnp.broadcast_to(start[0:1, j : j + 1], (PAN, 128))
        py = jnp.broadcast_to(start[1:2, j : j + 1], (PAN, 128))
        own_x = jnp.where(sub == j, px, own_x)
        own_y = jnp.where(sub == j, py, own_y)
        both = jnp.where(sub == 0, px, jnp.where(sub == 1, py, 0.0))
        mark = jnp.where(lane == (r % 16) * PAN + j, both, mark)
    pan[z, x, core, :, DEPTH:] = mark
    rows.wait()
    greeted()

    first = Gather(pan, *sems[:4])
    second = Gather(dgat, *sems[4:])

    def panel_copy(source, target):
        block = pan.at[source, x, core]
        return send(block, block, sz.at[target], rz.at[source], {"row": target * 8 + x * 2 + core})

    def panel_each(act):
        def ring(k, carry):
            @pl.when(z >= k)
            def _():
                act(panel_copy(z, z - k))

            @pl.when(z + k < NZ)
            def _():
                act(panel_copy(z, z + k))

            return carry

        lax.fori_loop(1, NZ, ring, 0)

    panel_each(lambda copy: copy.start())
    load.wait()

    def panel_fetch(source):
        @pl.when(source != z)
        def _():
            panel_copy(source, z).wait_recv()

    def split(k):
        @pl.when(k < 8)
        def _():
            fhigh[k // 2, k % 2], flow[k // 2, k % 2] = halves(fv[k // 2, k % 2])

    def arrived(source):
        at = pl.ds(pl.multiple_of(source * 64, 64), 64)
        high[at, :], low[at, :] = halves(pan[source, :, :, :, :DEPTH].reshape(64, DEPTH))

    first.run(lambda k: k, panel_fetch, split, arrived)

    def y_small(e):
        return send(dsmall, dy.at[e - 1], sdy.at[e - 1], rdy.at[e - 1], {"col": (c + e) % NCOL})

    def y_large(s, e):
        part = (c + e) % NCOL
        return send(u.at[part, s], ybuf.at[s, e - 1], sy.at[s, e - 1], ry.at[s, e - 1], {"col": part})

    ring_place = h * NZ + z

    def part_copy(source, target):
        block = dpart.at[source]
        return send(block, block, sdg.at[target], rdg.at[source],
                    {"gen": target // NZ, "row": target % NZ * 8 + x * 2 + core})

    def part_each(act):
        def ring(k, carry):
            act(part_copy(ring_place, (ring_place + k) % (2 * NZ)))

            @pl.when(k < NZ)
            def _():
                act(part_copy(ring_place, (ring_place + 2 * NZ - k) % (2 * NZ)))

            return carry

        lax.fori_loop(1, NZ + 1, ring, 0)

    def part_fetch(source):
        for g in range(2):
            @pl.when(ring_place != g * NZ + source)
            def _():
                part_copy(g * NZ + source, ring_place).wait_recv()

        dgat[source, x, core] = dpart[source] + dpart[NZ + source]

    gen_large = send(gout, gbuf, sg.at[0], rg.at[0], {"gen": 1 - h})

    def tile_of(i):
        return (z // 2 + i) % 4

    def multiply(s):
        a = [part[:, s].reshape(4 * HALF, DEPTH) for part in (fhigh, flow)]
        u[:, s] = three(a, (high[...], low[...])).reshape(4, HALF, B)

    top = [part[0, 0, :16] for part in (fhigh, flow)]
    rows8 = three(top, (high[...], low[...]))[:PAN]
    for q in range(4):
        dall[q] = rows8[:, 128 * q : 128 * q + 128]
    for i in range(3):
        dsmall[i] = dall[tile_of(i)]
    for e in range(1, NCOL):
        y_small(e).start()
    grouped = pan[:, :, :, :, DEPTH:].reshape(4, 16, PAN, 128)
    for q in range(4):
        total = grouped[q, 0]
        for i in range(1, 16):
            total = total + grouped[q, i]
        points[q] = total
    kern = []
    for i in range(3):
        marked = points[tile_of(i)]
        same = jnp.where(lane + 128 * tile_of(i) == sub + PAN * r, f32(nugget_term), f32(0))
        kern.append(matern(own_x - marked[0:1], own_y - marked[1:2]) + same)
    multiply(0)
    for e in range(1, NCOL):
        y_small(e).wait_recv()
    for i in range(3):
        total = dsmall[i] + dy[0, i] + dy[1, i] + dy[2, i]
        dpart[ring_place, i] = jnp.where(h == 0, kern[i], 0.0) - total
    part_each(lambda copy: copy.start())

    @pl.when(h == 1)
    def _():
        for e in range(1, NCOL):
            y_large(0, e).start()

    multiply(1)

    @pl.when(h == 0)
    def _():
        for e in range(1, NCOL):
            y_large(1, e).start()

    here = pl.ds(pl.multiple_of((c * 2 + h) * HALF, HALF), HALF)
    mx = jnp.broadcast_to(place_ref[0:1, here].astype(f32) / GRID, (HALF, HALF)).T
    my = jnp.broadcast_to(place_ref[1:2, here].astype(f32) / GRID, (HALF, HALF)).T
    isub = lax.broadcasted_iota(jnp.int32, (HALF, 128), 0) + (c * 2 + h) * HALF
    ilane = lax.broadcasted_iota(jnp.int32, (HALF, 128), 1)
    for q in range(4):
        at = slice(128 * q, 128 * q + 128)
        same = (isub < PAN) & (ilane + 128 * q == isub + PAN * r)
        k = matern(mx - points[q, 0:1], my - points[q, 1:2]) + jnp.where(same, f32(nugget_term), f32(0))
        upd[:, at] = k
    linv[...] = jnp.zeros((B, B), f32)
    def pass_on(k):
        @pl.when(k == NZ - 1)
        def _():
            for e in range(1, NCOL):
                y_large(1 - h, e).wait_recv()
            gout[...] = u[c, 1 - h] + ybuf[1 - h, 0] + ybuf[1 - h, 1] + ybuf[1 - h, 2]
            gen_large.start()
            for e in range(1, NCOL):
                y_large(h, e).start()

    second.run(lambda k: NZ // 2 + ((k + 1) // 2) * (1 - 2 * (k % 2)), part_fetch, pass_on, lag=1)
    for t, i in ((0, 0), (0, 1), (0, 2), (1, 0), (1, 1), (1, 2), (2, 0), (2, 1), (3, 0), (3, 1)):
        block = dgat[2 * t : 2 * t + 2, :, :, i].reshape(128, 128)
        if t + i == 4:
            block, row, col = block.T, 0, 3
        else:
            row, col = t, t + i
        work[128 * row : 128 * row + 128, 128 * col : 128 * col + 128] = block

    def combine():
        for e in range(1, NCOL):
            y_large(h, e).wait_recv()
        for q in range(4):
            at = slice(128 * q, 128 * q + 128)
            part = u[c, h, :, at] + ybuf[h, 0, :, at] + ybuf[h, 1, :, at] + ybuf[h, 2, :, at]
            upd[:, at] = upd[:, at] - part

    def settle():
        gen_large.wait_recv()
        upd[...] = upd[...] - gbuf[...]

    slot = c * 2 + h

    def deliver(g):
        return send(
            xs.at[g], xt.at[slot], sx.at[g], rx.at[slot], {"gen": g // NCOL, "col": g % NCOL}
        )

    def solve(v):
        lo, hi = 128 * v, 128 * v + 128
        block = dotf(linv[lo:hi, :hi], upd[:, :hi], ((1,), (1,)))
        for i in range(2):
            g = 2 * v + i
            xs[g] = block[64 * i : 64 * i + 64]

            @pl.when(h * NCOL + c == g)
            def _():
                xt[slot] = xs[g]

            @pl.when(h * NCOL + c != g)
            def _():
                deliver(g).start()

    def step(k, carry):
        for v in range(4):
            @pl.when(k == v)
            def _():
                tile[...] = work[128 * v : 128 * v + 128, 128 * v : 128 * v + 128]
        inverse_factor(tile, inv)
        for v in range(4):
            @pl.when(k == v)
            def _():
                lo, hi = 128 * v, 128 * v + 128
                t = inv[...]
                if v:
                    linv[lo:hi, :lo] = dotf(t, linv[lo:hi, :lo], ((1,), (0,)))
                linv[lo:hi, lo:hi] = t
                if v < 3:
                    p = dotf(t, work[lo:hi, hi:], ((1,), (0,)))
                    for w in range(v + 1, 4):
                        at = slice(128 * w, 128 * w + 128)
                        left = slice(128 * w - hi, 128 * w + 128 - hi)
                        work[at, 128 * w :] = work[at, 128 * w :] - dotf(p[:, left], p[:, 128 * w - hi :], ((0,), (0,)))
                    linv[hi:, :hi] = linv[hi:, :hi] - dotf(p, linv[lo:hi, :hi], ((0,), (0,)))
                if v == 1:
                    combine()
                    settle()
                    solve(0)
                if v:
                    solve(v)
        return carry

    lax.fori_loop(0, 4, step, 0)
    for e in range(1, NCOL):
        y_small(e).wait_send()
        for s in range(2):
            y_large(s, e).wait_send()
    part_each(lambda copy: copy.wait_send())
    panel_each(lambda copy: copy.wait_send())
    gen_large.wait_send()
    first.finish()
    second.finish()

    for g in range(2 * NCOL):
        @pl.when(h * NCOL + c != g)
        def _():
            theirs = (g % NCOL) * 2 + g // NCOL
            send(xs.at[g], xt.at[theirs], sx.at[g], rx.at[theirs], {"gen": g // NCOL, "col": g % NCOL}).wait_recv()

    for i in range(2 * NCOL):
        out[:, HALF * i : HALF * i + HALF] = xt[i]

    for g in range(2 * NCOL):
        @pl.when(h * NCOL + c != g)
        def _():
            deliver(g).wait_send()


def shards(coords, factor):
    dma = pltpu.SemaphoreType.DMA
    vmem = pl.BlockSpec(memory_space=pltpu.VMEM)

    def room(*shape, dtype=jnp.float32):
        return pltpu.VMEM(shape, dtype)

    solved = pl.pallas_call(
        step_kernel,
        out_shape=jax.ShapeDtypeStruct((B // 8, ROWS), jnp.float32),
        in_specs=[pl.BlockSpec(memory_space=pltpu.HBM)] * 2,
        out_specs=vmem,
        scratch_shapes=[
            room(2, ROWS, dtype=jnp.int32),
            room(4, 2, HALF, DEPTH),
            room(4, 2, HALF, DEPTH, dtype=jnp.bfloat16),
            room(4, 2, HALF, DEPTH, dtype=jnp.bfloat16),
            room(NZ, NX, NC, PAN, WIDE),
            room(B, DEPTH, dtype=jnp.bfloat16),
            room(B, DEPTH, dtype=jnp.bfloat16),
            room(4, 2, HALF, B),
            room(NZ, NX, NC, 3, PAN, 128),
            room(4, PAN, 128),
            room(3, PAN, 128),
            room(NCOL - 1, 3, PAN, 128),
            room(2 * NZ, 3, PAN, 128),
            room(2, NCOL - 1, HALF, B),
            room(HALF, B),
            room(HALF, B),
            room(4, PAN, 128),
            room(HALF, B),
            room(B, B),
            room(128, 128),
            room(128, 128),
            room(B, B),
            room(2 * NCOL, B // 8, HALF),
            room(2 * NCOL, B // 8, HALF),
            dma((4,)), dma((NZ,)), dma((NZ,)), dma((3,)), dma((3,)), dma((2 * NZ,)), dma((2 * NZ,)), dma((2, 3)), dma((2, 3)),
            dma((1,)), dma((1,)), dma((8,)), dma((8,)),
            *gather_sems(), *gather_sems(),
        ],
        compiler_params=pltpu.CompilerParams(
            collective_id=0, has_side_effects=True, vmem_limit_bytes=53 << 20
        ),
        name="panel_step",
    )(coords, factor.reshape(4, 2, HALF, DEPTH))
    return solved.T


def solution(mesh):
    in_specs = (P(None, "row"), P("row", ("gen", "col")))
    out_specs = P("row", ("gen", "col"))
    return jax.shard_map(shards, mesh=mesh, in_specs=in_specs, out_specs=out_specs, check_vma=False)
```

```python
import jax
import jax.numpy as jnp
from jax import lax
from jax.experimental import pallas as pl
from jax.experimental.pallas import tpu as pltpu
from jax.sharding import PartitionSpec as P

B = 512
GRID = 1024
PAN = 8
ROWS = 1024
DEPTH = 1024
HALF = 128
LAG = 2
NZ, NX, NC, NCOL = 8, 4, 2, 4
WIDE = DEPTH + 128

root_three = 1.7320508075688772
length_scale = 0.2
nugget_term = 1.0

HI = lax.Precision.HIGHEST
MESH = pl.DeviceIdType.MESH


def dotf(a, b, dims):
    return lax.dot_general(a, b, (dims, ((), ())), precision=HI, preferred_element_type=jnp.float32)


def matern(delta_x, delta_y):
    scaled = root_three * jnp.sqrt(delta_x * delta_x + delta_y * delta_y) / length_scale
    return (1.0 + scaled) * jnp.exp(-scaled)


def spread(x, k):
    return jnp.broadcast_to(x[k : k + 1], x.shape)


def inverse_factor(tile_ref, out_ref):
    sub = lax.broadcasted_iota(jnp.int32, (8, 128), 0)
    lane = lax.broadcasted_iota(jnp.int32, (8, 128), 1)
    a = [tile_ref[8 * i : 8 * i + 8, :] for i in range(16)]
    t = [jnp.where(lane == sub + 8 * i, jnp.float32(1), jnp.float32(0)) for i in range(16)]
    for b in range(16):
        cols = [jnp.broadcast_to(a[b][:, 8 * b + k : 8 * b + k + 1], (8, 128)) for k in range(8)]
        recip, cross, scale = [], [], jnp.ones((8, 128), jnp.float32)
        for k in range(8):
            pivot = spread(cols[k], k)
            r = 1.0 / pivot
            recip.append(r)
            scale = jnp.where(sub == k, pivot, scale)
            m = jnp.where(sub > k, cols[k] * r, 0.0)
            row = []
            for j in range(k + 1, 8):
                s = spread(cols[j], k)
                row.append(s)
                cols[j] = cols[j] - m * s
            cross.append(row)
            a[b] = a[b] - m * spread(a[b], k)
            t[b] = t[b] - m * spread(t[b], k)
        ua = [spread(a[b], k) for k in range(8)]
        ut = [spread(t[b], k) for k in range(8)]
        out_ref[8 * b : 8 * b + 8, :] = t[b] * lax.rsqrt(scale)
        inverse_pivots = jnp.ones((8, 128), jnp.float32)
        for k in range(8):
            inverse_pivots = jnp.where(sub == k, recip[k], inverse_pivots)
        scaled = a[b] * inverse_pivots
        for i in range(b + 1, min(b + 1 + 2, 16)):
            c = [jnp.broadcast_to(a[i][:, 8 * b + k : 8 * b + k + 1], (8, 128)) for k in range(8)]
            da = dt = None
            for k in range(8):
                m = c[k] * recip[k]
                for j in range(k + 1, 8):
                    c[j] = c[j] - m * cross[k][j - k - 1]
                da = m * ua[k] if da is None else da + m * ua[k]
                dt = m * ut[k] if dt is None else dt + m * ut[k]
            a[i] = a[i] - da
            t[i] = t[i] - dt
        if b + 1 + 2 < 16:
            hi = scaled.astype(jnp.bfloat16).astype(jnp.float32); r1 = scaled - hi
            mi = r1.astype(jnp.bfloat16).astype(jnp.float32); lo = r1 - mi
            both = jnp.concatenate([a[b], t[b]], axis=1)
            bh = both.astype(jnp.bfloat16).astype(jnp.float32); r2 = both - bh
            bm = r2.astype(jnp.bfloat16).astype(jnp.float32); bl = r2 - bm
            lhs = jnp.concatenate([hi, hi, mi, hi, lo, mi, hi, hi], axis=0).astype(jnp.bfloat16)
            rhs = jnp.concatenate([bh, bm, bh, bl, bh, bm, 0 * bh, 0 * bh], axis=0).astype(jnp.bfloat16)
            delta = lax.dot_general(lhs, rhs, (((0,), (0,)), ((), ())), preferred_element_type=jnp.float32)
            for i in range(b + 1 + 2, 16):
                a[i] = a[i] - delta[8 * i : 8 * i + 8, :128]
                t[i] = t[i] - delta[8 * i : 8 * i + 8, 128:]
def place():
    h, r, c = lax.axis_index("gen"), lax.axis_index("row"), lax.axis_index("col")
    return h, r, c, r // 8, (r // 2) % 4, r % 2


def send(src, dst, send_sem, recv_sem, where):
    return pltpu.make_async_remote_copy(
        src_ref=src, dst_ref=dst, send_sem=send_sem, recv_sem=recv_sem, device_id=where, device_id_type=MESH
    )


class Gather:
    def __init__(self, buf, sx, rx, sc, rc):
        self.buf, self.sx, self.rx, self.sc, self.rc = buf, sx, rx, sc, rc
        _, self.r, _, self.z, self.x, self.core = place()

    def along_x(self, source, e):
        target = (self.x + e) % NX
        block = self.buf.at[source, self.x, self.core]
        return send(block, block, self.sx.at[source, e - 1], self.rx.at[source, self.x],
                    {"row": self.z * 8 + target * 2 + self.core})

    def from_x(self, source, e):
        x = (self.x + e) % NX
        block = self.buf.at[source, x, self.core]
        return send(block, block, self.sx.at[source, 0], self.rx.at[source, x], {"row": self.r + 1 - 2 * self.core})

    def across(self, source, core):
        block = self.buf.at[source, :, core]
        return send(block, block, self.sc.at[source], self.rc.at[source], {"row": self.r + 1 - 2 * self.core})

    def run(self, away, fetch, aside, arrived=None):
        z = self.z

        def forward(source):
            fetch(source)
            for e in (2, 1, 3):
                self.along_x(source, e).start()

        def swap(source):
            for e in range(1, NX):
                self.from_x(source, e).wait_recv()
            self.across(source, self.core).start()

        def arrive(source):
            self.across(source, 1 - self.core).wait_recv()
            if arrived is not None:
                arrived(source)

        def visit(act, k):
            d = away(k)
            inside = (k >= 0) & (k < NZ)

            @pl.when(inside & (z >= d))
            def _():
                act(z - d)

            @pl.when(inside & (d > 0) & (z + d < NZ))
            def _():
                act(z + d)

        def ring(k, carry):
            visit(forward, k)
            aside(k)
            visit(swap, k - LAG)
            return carry

        def last(k, carry):
            visit(arrive, k)
            return carry

        lax.fori_loop(0, NZ + LAG, ring, 0)
        lax.fori_loop(0, NZ, last, 0)

    def finish(self):
        def drain(source, carry):
            for e in range(1, NX):
                self.along_x(source, e).wait_send()
            self.across(source, self.core).wait_send()
            return carry

        lax.fori_loop(0, NZ, drain, 0)


def gather_sems():
    dma = pltpu.SemaphoreType.DMA
    return [dma((NZ, NX - 1)), dma((NZ, NX)), dma((NZ,)), dma((NZ,))]


def greet():
    h, r, c, z, x, core = place()
    barrier = pltpu.get_barrier_semaphore()
    peers = [{"row": (z + d) % NZ * 8 + x * 2 + core} for d in range(1, NZ)]
    peers += [{"row": z * 8 + (x + e) % NX * 2 + core} for e in range(1, NX)]
    peers += [{"row": r + 1 - 2 * core}]
    peers += [{"col": (c + e) % NCOL} for e in range(1, NCOL)]
    peers += [{"gen": 1 - h, "col": (c + e) % NCOL} for e in range(NCOL)]
    peers += [{"gen": 1 - h, "row": (z + d) % NZ * 8 + x * 2 + core} for d in range(1, NZ)]
    for peer in peers:
        pl.semaphore_signal(barrier, inc=1, device_id=peer, device_id_type=MESH)
    return lambda: pl.semaphore_wait(barrier, len(peers))


def halves(x):
    high = x.astype(jnp.bfloat16)
    return high, (x - high.astype(jnp.float32)).astype(jnp.bfloat16)


def three(a, b):
    dims = (((1,), (1,)), ((), ()))
    f32 = jnp.float32
    total = lax.dot_general(a[0], b[1], dims, preferred_element_type=f32)
    total += lax.dot_general(a[1], b[0], dims, preferred_element_type=f32)
    return total + lax.dot_general(a[0], b[0], dims, preferred_element_type=f32)


def step_kernel(
    coords, factor, out, place_ref, fv, fhigh, flow, pan, high, low, u, dgat, dall, dsmall, dy, dpart, ybuf, gout, gbuf, points, upd,
    work, tile, inv, linv, xs, xt, local, sz, rz, sdy, rdy, sdg, rdg, sy, ry, sg, rg, sx, rx, *sems,
):
    h, r, c, z, x, core = place()
    f32 = jnp.float32
    load = pltpu.make_async_copy(factor, fv, local.at[0])
    rows = pltpu.make_async_copy(factor.at[0, 0, pl.ds(0, PAN), :], pan.at[z, x, core, :, pl.ds(0, DEPTH)], local.at[1])
    where = pltpu.make_async_copy(coords, place_ref, local.at[3])
    where.start()
    rows.start()
    load.start()
    greeted = greet()
    where.wait()

    sub = lax.broadcasted_iota(jnp.int32, (PAN, 128), 0)
    lane = lax.broadcasted_iota(jnp.int32, (PAN, 128), 1)
    start = place_ref[:, :128].astype(f32) / GRID
    mark = jnp.zeros((PAN, 128), f32)
    own_x, own_y = mark, mark
    for j in range(PAN):
        px = jnp.broadcast_to(start[0:1, j : j + 1], (PAN, 128))
        py = jnp.broadcast_to(start[1:2, j : j + 1], (PAN, 128))
        own_x = jnp.where(sub == j, px, own_x)
        own_y = jnp.where(sub == j, py, own_y)
        both = jnp.where(sub == 0, px, jnp.where(sub == 1, py, 0.0))
        mark = jnp.where(lane == (r % 16) * PAN + j, both, mark)
    pan[z, x, core, :, DEPTH:] = mark
    rows.wait()
    greeted()

    first = Gather(pan, *sems[:4])
    second = Gather(dgat, *sems[4:])

    def panel_copy(source, target):
        block = pan.at[source, x, core]
        return send(block, block, sz.at[target], rz.at[source], {"row": target * 8 + x * 2 + core})

    def panel_each(act):
        def ring(k, carry):
            @pl.when(z >= k)
            def _():
                act(panel_copy(z, z - k))

            @pl.when(z + k < NZ)
            def _():
                act(panel_copy(z, z + k))

            return carry

        lax.fori_loop(1, NZ, ring, 0)

    panel_each(lambda copy: copy.start())
    load.wait()

    def panel_fetch(source):
        @pl.when(source != z)
        def _():
            panel_copy(source, z).wait_recv()

    def split(k):
        @pl.when(k < 8)
        def _():
            fhigh[k // 2, k % 2], flow[k // 2, k % 2] = halves(fv[k // 2, k % 2])

    def arrived(source):
        at = pl.ds(pl.multiple_of(source * 64, 64), 64)
        high[at, :], low[at, :] = halves(pan[source, :, :, :, :DEPTH].reshape(64, DEPTH))

    first.run(lambda k: k, panel_fetch, split, arrived)

    def y_small(e):
        return send(dsmall, dy.at[e - 1], sdy.at[e - 1], rdy.at[e - 1], {"col": (c + e) % NCOL})

    def y_large(s, e):
        part = (c + e) % NCOL
        return send(u.at[part, s], ybuf.at[s, e - 1], sy.at[s, e - 1], ry.at[s, e - 1], {"col": part})

    ring_place = h * NZ + z

    def part_copy(source, target):
        block = dpart.at[source]
        return send(block, block, sdg.at[target], rdg.at[source],
                    {"gen": target // NZ, "row": target % NZ * 8 + x * 2 + core})

    def part_each(act):
        def ring(step, carry):
            k = NZ + 1 - step
            act(part_copy(ring_place, (ring_place + k) % (2 * NZ)))

            @pl.when(k < NZ)
            def _():
                act(part_copy(ring_place, (ring_place + 2 * NZ - k) % (2 * NZ)))

            return carry

        lax.fori_loop(1, NZ + 1, ring, 0)

    def part_fetch(source):
        for g in range(2):
            @pl.when(ring_place != g * NZ + source)
            def _():
                part_copy(g * NZ + source, ring_place).wait_recv()

        dgat[source, x, core] = dpart[source] + dpart[NZ + source]

    gen_large = send(gout, gbuf, sg.at[0], rg.at[0], {"gen": 1 - h})

    def tile_of(i):
        return (z // 2 + i) % 4

    def multiply(s):
        a = [part[:, s].reshape(4 * HALF, DEPTH) for part in (fhigh, flow)]
        u[:, s] = three(a, (high[...], low[...])).reshape(4, HALF, B)

    top = [part[0, 0, :16] for part in (fhigh, flow)]
    rows8 = three(top, (high[...], low[...]))[:PAN]
    for q in range(4):
        dall[q] = rows8[:, 128 * q : 128 * q + 128]
    for i in range(3):
        dsmall[i] = dall[tile_of(i)]
    for e in (2, 1, 3):
        y_small(e).start()
    grouped = pan[:, :, :, :, DEPTH:].reshape(4, 16, PAN, 128)
    for q in range(4):
        total = grouped[q, 0]
        for i in range(1, 16):
            total = total + grouped[q, i]
        points[q] = total
    kern = []
    for i in range(3):
        marked = points[tile_of(i)]
        same = jnp.where(lane + 128 * tile_of(i) == sub + PAN * r, f32(nugget_term), f32(0))
        kern.append(matern(own_x - marked[0:1], own_y - marked[1:2]) + same)
    multiply(0)
    for e in range(1, NCOL):
        y_small(e).wait_recv()
    for i in range(3):
        total = dsmall[i] + dy[0, i] + dy[1, i] + dy[2, i]
        dpart[ring_place, i] = jnp.where(h == 0, kern[i], 0.0) - total
    part_each(lambda copy: copy.start())

    @pl.when(h == 1)
    def _():
        for e in range(1, NCOL):
            y_large(0, e).start()

    multiply(1)

    @pl.when(h == 0)
    def _():
        for e in range(1, NCOL):
            y_large(1, e).start()

    here = pl.ds(pl.multiple_of((c * 2 + h) * HALF, HALF), HALF)
    mx = jnp.broadcast_to(place_ref[0:1, here].astype(f32) / GRID, (HALF, HALF)).T
    my = jnp.broadcast_to(place_ref[1:2, here].astype(f32) / GRID, (HALF, HALF)).T
    isub = lax.broadcasted_iota(jnp.int32, (HALF, 128), 0) + (c * 2 + h) * HALF
    ilane = lax.broadcasted_iota(jnp.int32, (HALF, 128), 1)
    for q in range(4):
        at = slice(128 * q, 128 * q + 128)
        same = (isub < PAN) & (ilane + 128 * q == isub + PAN * r)
        k = matern(mx - points[q, 0:1], my - points[q, 1:2]) + jnp.where(same, f32(nugget_term), f32(0))
        upd[:, at] = k
    linv[...] = jnp.zeros((B, B), f32)
    def pass_on(k):
        @pl.when(k == NZ - 1)
        def _():
            for e in range(1, NCOL):
                y_large(1 - h, e).wait_recv()
            gout[...] = u[c, 1 - h] + ybuf[1 - h, 0] + ybuf[1 - h, 1] + ybuf[1 - h, 2]
            gen_large.start()
            for e in range(1, NCOL):
                y_large(h, e).start()

    second.run(lambda k: NZ // 2 + ((k + 1) // 2) * (1 - 2 * (k % 2)), part_fetch, pass_on)
    for t, i in ((0, 0), (0, 1), (0, 2), (1, 0), (1, 1), (1, 2), (2, 0), (2, 1), (3, 0), (3, 1)):
        block = dgat[2 * t : 2 * t + 2, :, :, i].reshape(128, 128)
        if t + i == 4:
            block, row, col = block.T, 0, 3
        else:
            row, col = t, t + i
        work[128 * row : 128 * row + 128, 128 * col : 128 * col + 128] = block

    def combine():
        for e in range(1, NCOL):
            y_large(h, e).wait_recv()
        for q in range(4):
            at = slice(128 * q, 128 * q + 128)
            part = u[c, h, :, at] + ybuf[h, 0, :, at] + ybuf[h, 1, :, at] + ybuf[h, 2, :, at]
            upd[:, at] = upd[:, at] - part

    def settle():
        gen_large.wait_recv()
        upd[...] = upd[...] - gbuf[...]

    slot = c * 2 + h

    def deliver(g):
        return send(
            xs.at[g], xt.at[slot], sx.at[g], rx.at[slot], {"gen": g // NCOL, "col": g % NCOL}
        )

    def solve(v):
        lo, hi = 128 * v, 128 * v + 128
        block = dotf(linv[lo:hi, :hi], upd[:, :hi], ((1,), (1,)))
        for i in range(2):
            g = 2 * v + i
            xs[g] = block[64 * i : 64 * i + 64]

            @pl.when(h * NCOL + c == g)
            def _():
                xt[slot] = xs[g]

            @pl.when(h * NCOL + c != g)
            def _():
                deliver(g).start()

    def step(k, carry):
        for v in range(4):
            @pl.when(k == v)
            def _():
                tile[...] = work[128 * v : 128 * v + 128, 128 * v : 128 * v + 128]
        inverse_factor(tile, inv)
        for v in range(4):
            @pl.when(k == v)
            def _():
                lo, hi = 128 * v, 128 * v + 128
                t = inv[...]
                if v:
                    linv[lo:hi, :lo] = dotf(t, linv[lo:hi, :lo], ((1,), (0,)))
                linv[lo:hi, lo:hi] = t
                if v < 3:
                    p = dotf(t, work[lo:hi, hi:], ((1,), (0,)))
                    for w in range(v + 1, 4):
                        at = slice(128 * w, 128 * w + 128)
                        left = slice(128 * w - hi, 128 * w + 128 - hi)
                        work[at, 128 * w :] = work[at, 128 * w :] - dotf(p[:, left], p[:, 128 * w - hi :], ((0,), (0,)))
                    linv[hi:, :hi] = linv[hi:, :hi] - dotf(p, linv[lo:hi, :hi], ((0,), (0,)))
                if v == 1:
                    combine()
                    settle()
                    solve(0)
                if v:
                    solve(v)
        return carry

    lax.fori_loop(0, 4, step, 0)
    for e in range(1, NCOL):
        y_small(e).wait_send()
        for s in range(2):
            y_large(s, e).wait_send()
    part_each(lambda copy: copy.wait_send())
    panel_each(lambda copy: copy.wait_send())
    gen_large.wait_send()
    first.finish()
    second.finish()

    for g in range(2 * NCOL):
        @pl.when(h * NCOL + c != g)
        def _():
            theirs = (g % NCOL) * 2 + g // NCOL
            send(xs.at[g], xt.at[theirs], sx.at[g], rx.at[theirs], {"gen": g // NCOL, "col": g % NCOL}).wait_recv()

    for i in range(2 * NCOL):
        out[:, HALF * i : HALF * i + HALF] = xt[i]

    for g in range(2 * NCOL):
        @pl.when(h * NCOL + c != g)
        def _():
            deliver(g).wait_send()


def shards(coords, factor):
    dma = pltpu.SemaphoreType.DMA
    vmem = pl.BlockSpec(memory_space=pltpu.VMEM)

    def room(*shape, dtype=jnp.float32):
        return pltpu.VMEM(shape, dtype)

    solved = pl.pallas_call(
        step_kernel,
        out_shape=jax.ShapeDtypeStruct((B // 8, ROWS), jnp.float32),
        in_specs=[pl.BlockSpec(memory_space=pltpu.HBM)] * 2,
        out_specs=vmem,
        scratch_shapes=[
            room(2, ROWS, dtype=jnp.int32),
            room(4, 2, HALF, DEPTH),
            room(4, 2, HALF, DEPTH, dtype=jnp.bfloat16),
            room(4, 2, HALF, DEPTH, dtype=jnp.bfloat16),
            room(NZ, NX, NC, PAN, WIDE),
            room(B, DEPTH, dtype=jnp.bfloat16),
            room(B, DEPTH, dtype=jnp.bfloat16),
            room(4, 2, HALF, B),
            room(NZ, NX, NC, 3, PAN, 128),
            room(4, PAN, 128),
            room(3, PAN, 128),
            room(NCOL - 1, 3, PAN, 128),
            room(2 * NZ, 3, PAN, 128),
            room(2, NCOL - 1, HALF, B),
            room(HALF, B),
            room(HALF, B),
            room(4, PAN, 128),
            room(HALF, B),
            room(B, B),
            room(128, 128),
            room(128, 128),
            room(B, B),
            room(2 * NCOL, B // 8, HALF),
            room(2 * NCOL, B // 8, HALF),
            dma((4,)), dma((NZ,)), dma((NZ,)), dma((3,)), dma((3,)), dma((2 * NZ,)), dma((2 * NZ,)), dma((2, 3)), dma((2, 3)),
            dma((1,)), dma((1,)), dma((8,)), dma((8,)),
            *gather_sems(), *gather_sems(),
        ],
        compiler_params=pltpu.CompilerParams(
            collective_id=0, has_side_effects=True, vmem_limit_bytes=60 << 20
        ),
        name="panel_step",
    )(coords, factor.reshape(4, 2, HALF, DEPTH))
    return solved.T


def solution(mesh):
    in_specs = (P(None, "row"), P("row", ("gen", "col")))
    out_specs = P("row", ("gen", "col"))
    return jax.shard_map(shards, mesh=mesh, in_specs=in_specs, out_specs=out_specs, check_vma=False)
```

```python
import jax
import jax.numpy as jnp
from jax import lax
from jax.experimental import pallas as pl
from jax.experimental.pallas import tpu as pltpu
from jax.sharding import PartitionSpec as P

B = 512
GRID = 1024
PAN = 8
ROWS = 1024
DEPTH = 1024
HALF = 128
LAG = 2
NZ, NX, NC, NCOL = 8, 4, 2, 4
WIDE = DEPTH + 128

root_three = 1.7320508075688772
length_scale = 0.2
nugget_term = 1.0

HI = lax.Precision.HIGHEST
MESH = pl.DeviceIdType.MESH


def dotf(a, b, dims):
    return lax.dot_general(a, b, (dims, ((), ())), precision=HI, preferred_element_type=jnp.float32)


def matern(delta_x, delta_y):
    scaled = root_three * jnp.sqrt(delta_x * delta_x + delta_y * delta_y) / length_scale
    return (1.0 + scaled) * jnp.exp(-scaled)


def spread(x, k):
    return jnp.broadcast_to(x[k : k + 1], x.shape)


def inverse_factor(tile_ref, out_ref):
    sub = lax.broadcasted_iota(jnp.int32, (8, 128), 0)
    lane = lax.broadcasted_iota(jnp.int32, (8, 128), 1)
    a = [tile_ref[8 * i : 8 * i + 8, :] for i in range(16)]
    t = [jnp.where(lane == sub + 8 * i, jnp.float32(1), jnp.float32(0)) for i in range(16)]
    for b in range(16):
        cols = [jnp.broadcast_to(a[b][:, 8 * b + k : 8 * b + k + 1], (8, 128)) for k in range(8)]
        recip, cross, scale = [], [], jnp.ones((8, 128), jnp.float32)
        for k in range(8):
            pivot = spread(cols[k], k)
            r = 1.0 / pivot
            recip.append(r)
            scale = jnp.where(sub == k, pivot, scale)
            m = jnp.where(sub > k, cols[k] * r, 0.0)
            row = []
            for j in range(k + 1, 8):
                s = spread(cols[j], k)
                row.append(s)
                cols[j] = cols[j] - m * s
            cross.append(row)
            a[b] = a[b] - m * spread(a[b], k)
            t[b] = t[b] - m * spread(t[b], k)
        ua = [spread(a[b], k) for k in range(8)]
        ut = [spread(t[b], k) for k in range(8)]
        out_ref[8 * b : 8 * b + 8, :] = t[b] * lax.rsqrt(scale)
        inverse_pivots = jnp.ones((8, 128), jnp.float32)
        for k in range(8):
            inverse_pivots = jnp.where(sub == k, recip[k], inverse_pivots)
        scaled = a[b] * inverse_pivots
        for i in range(b + 1, min(b + 1 + 2, 16)):
            c = [jnp.broadcast_to(a[i][:, 8 * b + k : 8 * b + k + 1], (8, 128)) for k in range(8)]
            da = dt = None
            for k in range(8):
                m = c[k] * recip[k]
                for j in range(k + 1, 8):
                    c[j] = c[j] - m * cross[k][j - k - 1]
                da = m * ua[k] if da is None else da + m * ua[k]
                dt = m * ut[k] if dt is None else dt + m * ut[k]
            a[i] = a[i] - da
            t[i] = t[i] - dt
        if b + 1 + 2 < 16:
            hi = scaled.astype(jnp.bfloat16).astype(jnp.float32); r1 = scaled - hi
            mi = r1.astype(jnp.bfloat16).astype(jnp.float32); lo = r1 - mi
            both = jnp.concatenate([a[b], t[b]], axis=1)
            bh = both.astype(jnp.bfloat16).astype(jnp.float32); r2 = both - bh
            bm = r2.astype(jnp.bfloat16).astype(jnp.float32); bl = r2 - bm
            lhs = jnp.concatenate([hi, hi, mi, hi, lo, mi, hi, hi], axis=0).astype(jnp.bfloat16)
            rhs = jnp.concatenate([bh, bm, bh, bl, bh, bm, 0 * bh, 0 * bh], axis=0).astype(jnp.bfloat16)
            delta = lax.dot_general(lhs, rhs, (((0,), (0,)), ((), ())), preferred_element_type=jnp.float32)
            for i in range(b + 1 + 2, 16):
                a[i] = a[i] - delta[8 * i : 8 * i + 8, :128]
                t[i] = t[i] - delta[8 * i : 8 * i + 8, 128:]
def place():
    h, r, c = lax.axis_index("gen"), lax.axis_index("row"), lax.axis_index("col")
    return h, r, c, r // 8, (r // 2) % 4, r % 2


def send(src, dst, send_sem, recv_sem, where):
    return pltpu.make_async_remote_copy(
        src_ref=src, dst_ref=dst, send_sem=send_sem, recv_sem=recv_sem, device_id=where, device_id_type=MESH
    )


class Gather:
    def __init__(self, buf, sx, rx, sc, rc):
        self.buf, self.sx, self.rx, self.sc, self.rc = buf, sx, rx, sc, rc
        _, self.r, _, self.z, self.x, self.core = place()

    def along_x(self, source, e):
        target = (self.x + e) % NX
        block = self.buf.at[source, self.x, self.core]
        return send(block, block, self.sx.at[source, e - 1], self.rx.at[source, self.x],
                    {"row": self.z * 8 + target * 2 + self.core})

    def from_x(self, source, e):
        x = (self.x + e) % NX
        block = self.buf.at[source, x, self.core]
        return send(block, block, self.sx.at[source, 0], self.rx.at[source, x], {"row": self.r + 1 - 2 * self.core})

    def across(self, source, core):
        block = self.buf.at[source, :, core]
        return send(block, block, self.sc.at[source], self.rc.at[source], {"row": self.r + 1 - 2 * self.core})

    def run(self, away, fetch, aside, arrived=None):
        z = self.z

        def forward(source):
            fetch(source)
            for e in (2, 1, 3):
                self.along_x(source, e).start()

        def swap(source):
            for e in range(1, NX):
                self.from_x(source, e).wait_recv()
            self.across(source, self.core).start()

        def arrive(source):
            self.across(source, 1 - self.core).wait_recv()
            if arrived is not None:
                arrived(source)

        def visit(act, k):
            d = away(k)
            inside = (k >= 0) & (k < NZ)

            @pl.when(inside & (z >= d))
            def _():
                act(z - d)

            @pl.when(inside & (d > 0) & (z + d < NZ))
            def _():
                act(z + d)

        def ring(k, carry):
            visit(forward, k)
            aside(k)
            visit(swap, k - LAG)
            return carry

        def last(k, carry):
            visit(arrive, k)
            return carry

        lax.fori_loop(0, NZ + LAG, ring, 0)
        lax.fori_loop(0, NZ, last, 0)

    def finish(self):
        def drain(source, carry):
            for e in range(1, NX):
                self.along_x(source, e).wait_send()
            self.across(source, self.core).wait_send()
            return carry

        lax.fori_loop(0, NZ, drain, 0)


def gather_sems():
    dma = pltpu.SemaphoreType.DMA
    return [dma((NZ, NX - 1)), dma((NZ, NX)), dma((NZ,)), dma((NZ,))]


def greet():
    h, r, c, z, x, core = place()
    barrier = pltpu.get_barrier_semaphore()
    peers = [{"row": (z + d) % NZ * 8 + x * 2 + core} for d in range(1, NZ)]
    peers += [{"row": z * 8 + (x + e) % NX * 2 + core} for e in range(1, NX)]
    peers += [{"row": r + 1 - 2 * core}]
    peers += [{"col": (c + e) % NCOL} for e in range(1, NCOL)]
    peers += [{"gen": 1 - h, "col": (c + e) % NCOL} for e in range(NCOL)]
    peers += [{"gen": 1 - h, "row": (z + d) % NZ * 8 + x * 2 + core} for d in range(1, NZ)]
    for peer in peers:
        pl.semaphore_signal(barrier, inc=1, device_id=peer, device_id_type=MESH)
    return lambda: pl.semaphore_wait(barrier, len(peers))


def halves(x):
    high = x.astype(jnp.bfloat16)
    return high, (x - high.astype(jnp.float32)).astype(jnp.bfloat16)


def three(a, b):
    dims = (((1,), (1,)), ((), ()))
    f32 = jnp.float32
    total = lax.dot_general(a[0], b[1], dims, preferred_element_type=f32)
    total += lax.dot_general(a[1], b[0], dims, preferred_element_type=f32)
    return total + lax.dot_general(a[0], b[0], dims, preferred_element_type=f32)


def step_kernel(
    coords, factor, out, place_ref, fv, fhigh, flow, pan, high, low, u, dgat, dall, dsmall, dy, dpart, ybuf, gout, gbuf, points, upd,
    work, tile, inv, linv, xs, xt, local, sz, rz, sdy, rdy, sdg, rdg, sy, ry, sg, rg, sx, rx, *sems,
):
    h, r, c, z, x, core = place()
    f32 = jnp.float32
    load = pltpu.make_async_copy(factor, fv, local.at[0])
    rows = pltpu.make_async_copy(factor.at[0, 0, pl.ds(0, PAN), :], pan.at[z, x, core, :, pl.ds(0, DEPTH)], local.at[1])
    where = pltpu.make_async_copy(coords, place_ref, local.at[3])
    where.start()
    rows.start()
    load.start()
    greeted = greet()
    where.wait()

    sub = lax.broadcasted_iota(jnp.int32, (PAN, 128), 0)
    lane = lax.broadcasted_iota(jnp.int32, (PAN, 128), 1)
    start = place_ref[:, :128].astype(f32) / GRID
    mark = jnp.zeros((PAN, 128), f32)
    own_x, own_y = mark, mark
    for j in range(PAN):
        px = jnp.broadcast_to(start[0:1, j : j + 1], (PAN, 128))
        py = jnp.broadcast_to(start[1:2, j : j + 1], (PAN, 128))
        own_x = jnp.where(sub == j, px, own_x)
        own_y = jnp.where(sub == j, py, own_y)
        both = jnp.where(sub == 0, px, jnp.where(sub == 1, py, 0.0))
        mark = jnp.where(lane == (r % 16) * PAN + j, both, mark)
    pan[z, x, core, :, DEPTH:] = mark
    rows.wait()
    greeted()

    first = Gather(pan, *sems[:4])
    second = Gather(dgat, *sems[4:])

    def panel_copy(source, target):
        block = pan.at[source, x, core]
        return send(block, block, sz.at[target], rz.at[source], {"row": target * 8 + x * 2 + core})

    def panel_each(act):
        def ring(step, carry):
            k = NZ - step

            @pl.when(z >= k)
            def _():
                act(panel_copy(z, z - k))

            @pl.when(z + k < NZ)
            def _():
                act(panel_copy(z, z + k))

            return carry

        lax.fori_loop(1, NZ, ring, 0)

    panel_each(lambda copy: copy.start())
    load.wait()

    def panel_fetch(source):
        @pl.when(source != z)
        def _():
            panel_copy(source, z).wait_recv()

    def split(k):
        @pl.when(k < 8)
        def _():
            fhigh[k // 2, k % 2], flow[k // 2, k % 2] = halves(fv[k // 2, k % 2])

    def arrived(source):
        at = pl.ds(pl.multiple_of(source * 64, 64), 64)
        high[at, :], low[at, :] = halves(pan[source, :, :, :, :DEPTH].reshape(64, DEPTH))

    first.run(lambda k: (NZ - k) % NZ, panel_fetch, split, arrived)

    def y_small(e):
        return send(dsmall, dy.at[e - 1], sdy.at[e - 1], rdy.at[e - 1], {"col": (c + e) % NCOL})

    def y_large(s, e):
        part = (c + e) % NCOL
        return send(u.at[part, s], ybuf.at[s, e - 1], sy.at[s, e - 1], ry.at[s, e - 1], {"col": part})

    ring_place = h * NZ + z

    def part_copy(source, target):
        block = dpart.at[source]
        return send(block, block, sdg.at[target], rdg.at[source],
                    {"gen": target // NZ, "row": target % NZ * 8 + x * 2 + core})

    def part_each(act):
        def ring(step, carry):
            k = NZ + 1 - step
            act(part_copy(ring_place, (ring_place + k) % (2 * NZ)))

            @pl.when(k < NZ)
            def _():
                act(part_copy(ring_place, (ring_place + 2 * NZ - k) % (2 * NZ)))

            return carry

        lax.fori_loop(1, NZ + 1, ring, 0)

    def part_fetch(source):
        for g in range(2):
            @pl.when(ring_place != g * NZ + source)
            def _():
                part_copy(g * NZ + source, ring_place).wait_recv()

        dgat[source, x, core] = dpart[source] + dpart[NZ + source]

    gen_large = send(gout, gbuf, sg.at[0], rg.at[0], {"gen": 1 - h})

    def tile_of(i):
        return (z // 2 + i) % 4

    def multiply(s):
        a = [part[:, s].reshape(4 * HALF, DEPTH) for part in (fhigh, flow)]
        u[:, s] = three(a, (high[...], low[...])).reshape(4, HALF, B)

    top = [part[0, 0, :16] for part in (fhigh, flow)]
    rows8 = three(top, (high[...], low[...]))[:PAN]
    for q in range(4):
        dall[q] = rows8[:, 128 * q : 128 * q + 128]
    for i in range(3):
        dsmall[i] = dall[tile_of(i)]
    for e in (2, 1, 3):
        y_small(e).start()
    grouped = pan[:, :, :, :, DEPTH:].reshape(4, 16, PAN, 128)
    for q in range(4):
        total = grouped[q, 0]
        for i in range(1, 16):
            total = total + grouped[q, i]
        points[q] = total
    kern = []
    for i in range(3):
        marked = points[tile_of(i)]
        same = jnp.where(lane + 128 * tile_of(i) == sub + PAN * r, f32(nugget_term), f32(0))
        kern.append(matern(own_x - marked[0:1], own_y - marked[1:2]) + same)
    multiply(0)
    for e in range(1, NCOL):
        y_small(e).wait_recv()
    for i in range(3):
        total = dsmall[i] + dy[0, i] + dy[1, i] + dy[2, i]
        dpart[ring_place, i] = jnp.where(h == 0, kern[i], 0.0) - total
    part_each(lambda copy: copy.start())

    @pl.when(h == 1)
    def _():
        for e in range(1, NCOL):
            y_large(0, e).start()

    multiply(1)

    @pl.when(h == 0)
    def _():
        for e in range(1, NCOL):
            y_large(1, e).start()

    here = pl.ds(pl.multiple_of((c * 2 + h) * HALF, HALF), HALF)
    mx = jnp.broadcast_to(place_ref[0:1, here].astype(f32) / GRID, (HALF, HALF)).T
    my = jnp.broadcast_to(place_ref[1:2, here].astype(f32) / GRID, (HALF, HALF)).T
    isub = lax.broadcasted_iota(jnp.int32, (HALF, 128), 0) + (c * 2 + h) * HALF
    ilane = lax.broadcasted_iota(jnp.int32, (HALF, 128), 1)
    for q in range(4):
        at = slice(128 * q, 128 * q + 128)
        same = (isub < PAN) & (ilane + 128 * q == isub + PAN * r)
        k = matern(mx - points[q, 0:1], my - points[q, 1:2]) + jnp.where(same, f32(nugget_term), f32(0))
        upd[:, at] = k
    linv[...] = jnp.zeros((B, B), f32)
    def pass_on(k):
        @pl.when(k == NZ - 1)
        def _():
            for e in range(1, NCOL):
                y_large(1 - h, e).wait_recv()
            gout[...] = u[c, 1 - h] + ybuf[1 - h, 0] + ybuf[1 - h, 1] + ybuf[1 - h, 2]
            gen_large.start()
            for e in range(1, NCOL):
                y_large(h, e).start()

    second.run(lambda k: NZ // 2 + ((k + 1) // 2) * (1 - 2 * (k % 2)), part_fetch, pass_on)
    for t, i in ((0, 0), (0, 1), (0, 2), (1, 0), (1, 1), (1, 2), (2, 0), (2, 1), (3, 0), (3, 1)):
        block = dgat[2 * t : 2 * t + 2, :, :, i].reshape(128, 128)
        if t + i == 4:
            block, row, col = block.T, 0, 3
        else:
            row, col = t, t + i
        work[128 * row : 128 * row + 128, 128 * col : 128 * col + 128] = block

    def combine():
        for e in range(1, NCOL):
            y_large(h, e).wait_recv()
        for q in range(4):
            at = slice(128 * q, 128 * q + 128)
            part = u[c, h, :, at] + ybuf[h, 0, :, at] + ybuf[h, 1, :, at] + ybuf[h, 2, :, at]
            upd[:, at] = upd[:, at] - part

    def settle():
        gen_large.wait_recv()
        upd[...] = upd[...] - gbuf[...]

    slot = c * 2 + h

    def deliver(g):
        return send(
            xs.at[g], xt.at[slot], sx.at[g], rx.at[slot], {"gen": g // NCOL, "col": g % NCOL}
        )

    def solve(v):
        lo, hi = 128 * v, 128 * v + 128
        block = dotf(linv[lo:hi, :hi], upd[:, :hi], ((1,), (1,)))
        for i in range(2):
            g = 2 * v + i
            xs[g] = block[64 * i : 64 * i + 64]

            @pl.when(h * NCOL + c == g)
            def _():
                xt[slot] = xs[g]

            @pl.when(h * NCOL + c != g)
            def _():
                deliver(g).start()

    def step(k, carry):
        for v in range(4):
            @pl.when(k == v)
            def _():
                tile[...] = work[128 * v : 128 * v + 128, 128 * v : 128 * v + 128]
        inverse_factor(tile, inv)
        for v in range(4):
            @pl.when(k == v)
            def _():
                lo, hi = 128 * v, 128 * v + 128
                t = inv[...]
                if v:
                    linv[lo:hi, :lo] = dotf(t, linv[lo:hi, :lo], ((1,), (0,)))
                linv[lo:hi, lo:hi] = t
                if v < 3:
                    p = dotf(t, work[lo:hi, hi:], ((1,), (0,)))
                    for w in range(v + 1, 4):
                        at = slice(128 * w, 128 * w + 128)
                        left = slice(128 * w - hi, 128 * w + 128 - hi)
                        work[at, 128 * w :] = work[at, 128 * w :] - dotf(p[:, left], p[:, 128 * w - hi :], ((0,), (0,)))
                    linv[hi:, :hi] = linv[hi:, :hi] - dotf(p, linv[lo:hi, :hi], ((0,), (0,)))
                if v == 1:
                    combine()
                    settle()
                    solve(0)
                if v:
                    solve(v)
        return carry

    lax.fori_loop(0, 4, step, 0)
    for e in range(1, NCOL):
        y_small(e).wait_send()
        for s in range(2):
            y_large(s, e).wait_send()
    part_each(lambda copy: copy.wait_send())
    panel_each(lambda copy: copy.wait_send())
    gen_large.wait_send()
    first.finish()
    second.finish()

    for g in range(2 * NCOL):
        @pl.when(h * NCOL + c != g)
        def _():
            theirs = (g % NCOL) * 2 + g // NCOL
            send(xs.at[g], xt.at[theirs], sx.at[g], rx.at[theirs], {"gen": g // NCOL, "col": g % NCOL}).wait_recv()

    for i in range(2 * NCOL):
        out[:, HALF * i : HALF * i + HALF] = xt[i]

    for g in range(2 * NCOL):
        @pl.when(h * NCOL + c != g)
        def _():
            deliver(g).wait_send()


def shards(coords, factor):
    dma = pltpu.SemaphoreType.DMA
    vmem = pl.BlockSpec(memory_space=pltpu.VMEM)

    def room(*shape, dtype=jnp.float32):
        return pltpu.VMEM(shape, dtype)

    solved = pl.pallas_call(
        step_kernel,
        out_shape=jax.ShapeDtypeStruct((B // 8, ROWS), jnp.float32),
        in_specs=[pl.BlockSpec(memory_space=pltpu.HBM)] * 2,
        out_specs=vmem,
        scratch_shapes=[
            room(2, ROWS, dtype=jnp.int32),
            room(4, 2, HALF, DEPTH),
            room(4, 2, HALF, DEPTH, dtype=jnp.bfloat16),
            room(4, 2, HALF, DEPTH, dtype=jnp.bfloat16),
            room(NZ, NX, NC, PAN, WIDE),
            room(B, DEPTH, dtype=jnp.bfloat16),
            room(B, DEPTH, dtype=jnp.bfloat16),
            room(4, 2, HALF, B),
            room(NZ, NX, NC, 3, PAN, 128),
            room(4, PAN, 128),
            room(3, PAN, 128),
            room(NCOL - 1, 3, PAN, 128),
            room(2 * NZ, 3, PAN, 128),
            room(2, NCOL - 1, HALF, B),
            room(HALF, B),
            room(HALF, B),
            room(4, PAN, 128),
            room(HALF, B),
            room(B, B),
            room(128, 128),
            room(128, 128),
            room(B, B),
            room(2 * NCOL, B // 8, HALF),
            room(2 * NCOL, B // 8, HALF),
            dma((4,)), dma((NZ,)), dma((NZ,)), dma((3,)), dma((3,)), dma((2 * NZ,)), dma((2 * NZ,)), dma((2, 3)), dma((2, 3)),
            dma((1,)), dma((1,)), dma((8,)), dma((8,)),
            *gather_sems(), *gather_sems(),
        ],
        compiler_params=pltpu.CompilerParams(
            collective_id=0, has_side_effects=True, vmem_limit_bytes=60 << 20
        ),
        name="panel_step",
    )(coords, factor.reshape(4, 2, HALF, DEPTH))
    return solved.T


def solution(mesh):
    in_specs = (P(None, "row"), P("row", ("gen", "col")))
    out_specs = P("row", ("gen", "col"))
    return jax.shard_map(shards, mesh=mesh, in_specs=in_specs, out_specs=out_specs, check_vma=False)
```
